32 devices in a mesh: groups: 2 (over y), chan: 4 (over z), tm: 2 (over x), sub: 2 (over core).
Axes of the slice: x: 2, y: 2, z: 4, core: 2. Of those that a mesh axis runs over, the one named last changes fastest.
Arguments:
- traces: float32 [2048, 8192], P(('groups', 'chan', 'sub'), 'tm'), parts along dimension 0, may hold values from -6 to 6
- filters: float32 [2048, 65], P(('groups', 'chan', 'sub')), parts along dimension 0, may hold values from -0.75 to 0.75
- sources: int32 [256], P('groups'), parts along dimension 0, may hold values from 0 to 1023, as said below
Outputs:
- corr: float32 [128, 129, 2048], P('tm', None, ('groups', 'chan', 'sub')), parts along dimension 2
The draws below stay inside these ranges and needn't reach their ends.
There are 2 independent parts, one for each index of `groups`. The reference program is written for one: setup_inputs(seed, part) draws one part's arguments, and reference() takes and returns one part's arrays. A program takes and returns all parts, laid end to end along the dimension named above; each array names one. Nothing has to cross between parts.
Inputs may be any that keep to these rules, and one draw needn't show every extreme that they name: `sources`: the 128 partner channels are distinct. No block of 128 consecutive channels starting at a multiple of 128 holds more than 16 of them, and some block holds exactly 16.
All inputs are finite; a program needn't handle non-finite values.
Results may differ from the reference program's by a relative error of at most 0.0033.
Values may be sent and summed in bfloat16 or wider, within the bound.
No kernel may reach another device: no remote copies, remote signals or barrier semaphores. Data moves between devices by JAX's collectives and lax.ppermute only.
A program may use at most 64 MiB of HBM per device.

```python
import math
import jax
import jax.numpy as jnp
from jax import lax

C = 1024
P_SIZE = 128
TAPS = 65
LAGS = 129
CB = 128
MOST = 16
SAMPLES = 8192


def draw_sources(key, part):
    blocks = C // CB
    key_head, key_order, key_prefer, key_noise, key_shuffle = jax.random.split(jax.random.fold_in(key, 17), 5)
    head_block = jax.random.randint(key_head, (), 0, blocks)
    order_scores = jax.random.randint(key_order, (blocks, CB), 0, 65536) * CB + jnp.arange(CB, dtype=jnp.int32)[None, :]
    within = jnp.argsort(order_scores, axis=1, stable=True)[:, :MOST]
    slot_chan = jnp.arange(blocks, dtype=jnp.int32)[:, None] * CB + within
    prefer = jax.random.randint(key_prefer, (blocks, 1), 0, 4)
    noise_part = jax.random.randint(key_noise, (blocks, MOST), 0, 2048)
    slot_index = jnp.arange(blocks * MOST, dtype=jnp.int32).reshape(blocks, MOST)
    scores = (prefer * 2048 + noise_part) * (blocks * MOST) + slot_index
    is_head = jnp.arange(blocks, dtype=jnp.int32)[:, None] == head_block
    scores = jnp.where(is_head, 8192 * blocks * MOST + slot_index, scores)
    top_values, chosen = lax.top_k(scores.reshape(-1), P_SIZE)
    picked = slot_chan.reshape(-1)[chosen]
    shuffle = jax.random.randint(key_shuffle, (P_SIZE,), 0, 65536) * P_SIZE + jnp.arange(P_SIZE, dtype=jnp.int32)
    return picked[jnp.argsort(shuffle, stable=True)].astype(jnp.int32)


def levels(stream_key, shape, cuts, least, high):
    loudness, own = 1.0, jax.random.fold_in(stream_key, 6)
    for position, blocks in cuts:
        draws = jnp.exp(jax.random.uniform(jax.random.fold_in(own, position), (blocks,), jnp.float32, least / len(cuts), high / len(cuts)))
        loudness = loudness * jnp.repeat(draws, shape[position] // blocks).reshape([-1 if axis == position else 1 for axis in range(len(shape))])
    return loudness


def noise(own_key, dims, width, reach, pieces=(), kind=jnp.bfloat16):
    level = levels(own_key, dims, pieces, -0.22, 0.18) if pieces else 1.0
    drawn = jax.random.normal(own_key, dims, jnp.float32) * width * level
    return jnp.minimum(jnp.maximum(drawn, -reach), reach).astype(kind)


def setup_inputs(seed: int = 0, part: int = 0) -> dict:
    key_of = jax.random.split(jax.random.key(seed), 4)
    part_keys = jax.random.split(jax.random.fold_in(key_of[3], part), 4)
    traces = noise(part_keys[0], (C, SAMPLES), 1.0, 6.0, ((0, 8), (1, 2)), jnp.float32)
    filters = noise(part_keys[1], (C, TAPS), TAPS ** -0.5, 0.75, ((0, 8),), jnp.float32)
    sources = draw_sources(jax.random.fold_in(jax.random.fold_in(key_of[3], part), 71), part)
    return dict(traces=traces, filters=filters, sources=sources)


def reference(traces, filters, sources):
    num_samples = traces.shape[1]
    half_taps = (TAPS - 1) // 2
    extended = jnp.pad(traces, ((0, 0), (half_taps, half_taps)))
    running = jnp.zeros(traces.shape, jnp.float32)
    for k in range(TAPS):
        running = running + filters[:, k:k + 1] * extended[:, k:k + num_samples]
    whitened = running.astype(jnp.bfloat16)
    partner_traces = whitened[sources]
    half_lags = (LAGS - 1) // 2
    padded = jnp.pad(whitened.astype(jnp.float32), ((0, 0), (half_lags, half_lags)))
    partner_float = partner_traces.astype(jnp.float32)

    def one_lag(lag_index):
        first_col = (LAGS - 1 - lag_index).astype(jnp.int32)
        shifted = lax.dynamic_slice_in_dim(padded, first_col, num_samples, 1)
        return jnp.dot(partner_float, shifted.T, precision=lax.Precision.HIGHEST)
    stacked = lax.map(one_lag, jnp.arange(LAGS, dtype=jnp.int32))
    norm_scale = 1.0 / math.sqrt(SAMPLES)
    return jnp.transpose(stacked, (1, 0, 2)) * norm_scale
```

```python
import functools
import math

import jax
import jax.numpy as jnp
from jax import lax
from jax.experimental import pallas as pl
from jax.experimental.pallas import tpu as pltpu
from jax.sharding import PartitionSpec as P

LAGS = 129
MOST = 16
TILE = 128
FINE = 16
F32 = jnp.float32
BF16 = jnp.bfloat16
VMEM_BYTES = 56 * 2**20


def vmem(count):
    return [pl.BlockSpec(memory_space=pltpu.VMEM)] * count


SMEM = pl.BlockSpec(memory_space=pltpu.SMEM)
ANY = pl.BlockSpec(memory_space=pl.ANY)


def params():
    return pltpu.CompilerParams(vmem_limit_bytes=VMEM_BYTES)


def cost(flops, moved):
    return pl.CostEstimate(flops=int(flops), bytes_accessed=int(moved), transcendentals=0)


def fir(samples, taps_ref, taps, base, rows):
    total = None
    for first in range(8):
        later = [j for j in range((taps + 7) // 8) if first + 8 * j < taps]
        window = samples[pl.ds(base + first, rows + 8 * later[-1]), :]
        for j in later:
            k = first + 8 * j
            term = taps_ref[k : k + 1, :] * window[8 * j : 8 * j + rows]
            total = term if total is None else total + term
    return total


def slots_kernel(taps, sources, info, x, low, high, filters, out, rows, wide, tall, chan_taps, lane_taps):
    chans, length = x.shape
    slots = out.shape[0]
    segs = TILE // slots
    seg_len = length // segs
    half = (taps - 1) // 2
    for s in range(slots):
        rows[s] = 0

    def find(p, count):
        local = sources[p] - info[0] * chans
        mine = (local >= 0) & (local < chans)
        rows[jnp.where(mine, count, slots)] = local
        return count + mine.astype(jnp.int32)

    lax.fori_loop(0, sources.shape[0], find, 0, unroll=8)
    lane_taps[0:taps, :chans] = filters[...]
    chan_taps[...] = lane_taps[:, :chans].T
    keep_low = (info[1] > 0).astype(F32)
    keep_high = (info[2] > 0).astype(F32)
    for s in range(slots):
        row = rows[s]
        group = pl.multiple_of((row >> 3) << 3, 8)
        turn = (s - row) & 7

        def pick(ref):
            return pltpu.roll(ref[pl.ds(group, 8), :], turn, 0)[s % 8 : s % 8 + 1, :]

        wide[s : s + 1, 0:TILE] = pick(low) * keep_low
        wide[s : s + 1, TILE : TILE + length] = pick(x)
        wide[s : s + 1, TILE + length :] = pick(high) * keep_high
        lane_taps[s : s + 1, :] = pick(chan_taps)
    picked = lane_taps[0:slots, :]
    lane_taps[...] = jnp.concatenate([picked] * segs, 0).T
    for t in range(seg_len // TILE + 2):
        cols = [wide[:, g * seg_len + t * TILE : g * seg_len + (t + 1) * TILE] for g in range(segs)]
        tall[t * TILE : (t + 1) * TILE, :] = jnp.concatenate(cols, 0).T
    for t in range(seg_len // TILE):
        done = fir(tall, lane_taps, taps, (t + 1) * TILE - half, TILE).T
        for g in range(segs):
            start = g * seg_len + t * TILE
            out[:, start : start + TILE] = done[g * slots : (g + 1) * slots].astype(BF16)


def whiten_slots(sources, info, traces, low, high, filters, slots):
    chans, length = traces.shape
    taps = filters.shape[0]
    seg_len = length * slots // TILE
    return pl.pallas_call(
        functools.partial(slots_kernel, taps),
        out_shape=jax.ShapeDtypeStruct((slots, length), BF16),
        in_specs=[SMEM, SMEM] + vmem(4),
        out_specs=vmem(1)[0],
        scratch_shapes=[
            pltpu.SMEM((slots + 1,), jnp.int32),
            pltpu.VMEM((slots, length + 2 * TILE), F32),
            pltpu.VMEM((seg_len + 2 * TILE, TILE), F32),
            pltpu.VMEM((chans, TILE), F32),
            pltpu.VMEM((TILE, TILE), F32),
        ],
        compiler_params=params(),
        cost_estimate=cost(2 * slots * length * taps, 4 * chans * length),
        name="whiten_slots",
    )(sources, info, traces, low, high, filters)


def whiten_kernel(taps, rows, info, x, low, high, filters, out, tall):
    length = x.shape[1]
    half = (taps - 1) // 2
    tall[0:TILE, :] = jnp.where(info[1] > 0, low[...], 0.0).T
    tall[TILE + length :, :] = jnp.where(info[2] > 0, high[...], 0.0).T

    def turn(t, carry):
        start = pl.multiple_of(t * TILE, TILE)
        tall[pl.ds(start + TILE, TILE), :] = x[:, pl.ds(start, TILE)].T
        return carry

    lax.fori_loop(0, length // TILE, turn, 0, unroll=4)

    def block(i, carry):
        start = pl.multiple_of(i * rows, rows)
        out[pl.ds(start, rows), :] = fir(tall, filters, taps, start + TILE - half, rows).astype(BF16)
        return carry

    lax.fori_loop(0, length // rows, block, 0)


def whiten(info, traces, low, high, filters):
    chans, length = traces.shape
    taps = filters.shape[0]
    return pl.pallas_call(
        functools.partial(whiten_kernel, taps, 2 * TILE),
        out_shape=jax.ShapeDtypeStruct((length, chans), BF16),
        in_specs=[SMEM] + vmem(4),
        out_specs=vmem(1)[0],
        scratch_shapes=[pltpu.VMEM((length + 2 * TILE, chans), F32)],
        compiler_params=params(),
        cost_estimate=cost(2 * chans * length * taps, 6 * chans * length),
        name="whiten",
    )(info, traces, low, high, filters)


def order_kernel(chans, sizes, ring, count, lead, send_rows, info, sources, *refs):
    parts, outs = refs[:count], refs[count : -2]
    slots_ref, choose = refs[-2:]
    partners = sources.shape[1]
    chan_devs, sub_devs = sizes
    slots = parts[0].shape[0] if ring else MOST
    own_row = jnp.broadcast_to(sources[...].astype(F32), (partners, partners))
    owner_row = jnp.floor((own_row + 0.5) * (1.0 / chans))
    owner_col = owner_row.T
    lane = lax.broadcasted_iota(jnp.int32, (partners, partners), 1)
    line = lax.broadcasted_iota(jnp.int32, (partners, partners), 0)
    earlier = (owner_row == owner_col) & (lane < line)
    rank = jnp.sum(earlier.astype(F32), axis=1, keepdims=True)
    owner = owner_col[:, 0:1]
    if ring:
        owner_chan = jnp.floor((owner + 0.5) * (1.0 / sub_devs))
        owner_sub = owner - sub_devs * owner_chan
        my_chan = info[3].astype(F32)
        my_sub = info[4].astype(F32)
        behind = my_chan - owner_chan
        behind = jnp.where(behind < 0, behind + chan_devs, behind)
        place = jnp.where(owner_sub == my_sub, 0.0, 1.0) * chan_devs + behind
    else:
        place = owner
    row = place * slots + rank
    total = slots_ref.shape[0]
    at = lax.broadcasted_iota(jnp.int32, (partners, total), 1).astype(F32)
    choose[...] = (row == at).astype(F32)
    step = total // count
    for i, part in enumerate(parts):
        slots_ref[i * step : (i + 1) * step, :] = part[...]
    if not ring:
        outs[0][...] = jnp.dot(choose[...].astype(BF16), slots_ref[...], preferred_element_type=F32).astype(BF16)
        return
    own, send = outs
    half = own.shape[0]
    mine = choose[pl.ds(pl.multiple_of(info[5] * half, half), half), :]
    other = (1 - info[5]) * half + info[4] * send_rows
    theirs = choose[pl.ds(pl.multiple_of(other, send_rows), send_rows), :]
    wanted = jnp.concatenate([mine, theirs], 0).astype(BF16)
    length = send.shape[1]
    got = jnp.dot(wanted, slots_ref[...], preferred_element_type=F32).astype(BF16)
    own[:, 0:lead] = jnp.zeros((half, lead), BF16)
    own[:, lead + length :] = jnp.zeros((half, lead), BF16)
    own[:, lead : lead + length] = got[:half]
    send[...] = got[half:]


def order(info, sources, parts, chans, sizes, ring):
    partners = sources.shape[0]
    length = parts[0].shape[1]
    total = sum(part.shape[0] for part in parts)
    if ring:
        half, send_rows = partners // 2, partners // 4
        out_shape = (
            jax.ShapeDtypeStruct((half, length + 2 * TILE), BF16),
            jax.ShapeDtypeStruct((send_rows, length), BF16),
        )
        out_specs = tuple(vmem(2))
    else:
        send_rows = 0
        out_shape = jax.ShapeDtypeStruct((partners, length), BF16)
        out_specs = vmem(1)[0]
    return pl.pallas_call(
        functools.partial(order_kernel, chans, sizes, ring, len(parts), TILE, send_rows),
        out_shape=out_shape,
        in_specs=[SMEM] + vmem(1 + len(parts)),
        out_specs=out_specs,
        scratch_shapes=[pltpu.VMEM((total, length), BF16), pltpu.VMEM((partners, total), F32)],
        compiler_params=params(),
        cost_estimate=cost(2 * partners * total * length, 4 * total * length),
        name="order_partners",
    )(info, sources.reshape(1, partners), *parts)


def lay_out(part, out, start, width):
    rows = part.shape[0]
    lane = lax.broadcasted_iota(jnp.int32, (rows, TILE), 1)
    tiles = [part[:, pl.ds(start + TILE * i, TILE)] for i in range(width // TILE + 1)]
    half = (LAGS - 1) // 2
    for b in range(FINE + 1):
        turned = [pltpu.roll(tile, half - b, 1) for tile in tiles]
        for i in range(width // TILE):
            piece = jnp.where(lane < half - b, turned[i], turned[i + 1])
            out[b * rows : (b + 1) * rows, TILE * i : TILE * i + TILE] = piece


def add_lags(shifted, chan, total, start, width, rows):
    chans = chan.shape[1]
    coarse = (LAGS - 1) // FINE
    pair = 2 if chans % TILE == 0 else 1
    for a in range(0, coarse, pair):
        cols = [chan[pl.ds(start + TILE - FINE * (a + i), width), :] for i in range(pair)]
        last = a + pair == coarse
        used = rows * (FINE + 1 if last else FINE)
        block = cols[0] if pair == 1 else jnp.concatenate(cols, 1)
        term = jnp.dot(shifted[:used, :], block, preferred_element_type=F32)
        for i in range(pair):
            size = used if i == pair - 1 else rows * FINE
            place = (a + i) * FINE * rows
            total[place : place + size, :] += term[:size, i * chans : (i + 1) * chans]


def correlate_all(part, chan, total, spare, start, width, chunk, rows):
    first, second, rest = spare
    whole = width // (2 * chunk) * (2 * chunk)
    lay_out(part, first, start, chunk)

    def advance(i, carry):
        now = pl.multiple_of(start + 2 * chunk * i, TILE)
        lay_out(part, second, now + chunk, chunk)
        add_lags(first, chan, total, now, chunk, rows)
        after = pl.multiple_of(jnp.minimum(now + 2 * chunk, start + whole - chunk), TILE)
        lay_out(part, first, after, chunk)
        add_lags(second, chan, total, now + chunk, chunk, rows)
        return carry

    lax.fori_loop(0, whole // (2 * chunk), advance, 0)
    if width > whole:
        lay_out(part, rest, start + whole, width - whole)
        add_lags(rest, chan, total, start + whole, width - whole, rows)


def first_kernel(chunk, info, part, chan_hbm, total, chan, a, b, c, sem):
    length = chan_hbm.shape[0]
    rows = part.shape[0]
    copy = pltpu.make_async_copy(chan_hbm, chan.at[pl.ds(TILE, length), :], sem)
    copy.start()
    edge = jnp.zeros((TILE, chan.shape[1]), BF16)
    chan[0:TILE, :] = edge
    chan[TILE + length :, :] = edge
    total[...] = jnp.zeros_like(total)
    copy.wait()
    start = pl.multiple_of(info[5] * TILE, TILE)
    correlate_all(part, chan, total, (a, b, c), start, length, chunk, rows)


def second_kernel(chunk, scale, info, own_part, parts_hbm, own_chan, chan_hbm, before, total, part, chan, a, b, c, sems):
    length = chan_hbm.shape[0]
    rows = part.shape[0]
    few = parts_hbm[0].shape[0]
    copies = [
        pltpu.make_async_copy(parts_hbm[0], part.at[pl.ds(pl.multiple_of(info[6], few), few), pl.ds(TILE, length)], sems.at[0]),
        pltpu.make_async_copy(parts_hbm[1], part.at[pl.ds(pl.multiple_of(info[7], few), few), pl.ds(TILE, length)], sems.at[1]),
        pltpu.make_async_copy(chan_hbm, chan.at[pl.ds(TILE, length), :], sems.at[2]),
        pltpu.make_async_copy(before, total, sems.at[3]),
    ]
    for copy in copies:
        copy.start()
    later = info[5] > 0
    part[:, 0:TILE] = jnp.where(later, 0, own_part[:, length : length + TILE]).astype(BF16)
    part[:, TILE + length :] = jnp.where(later, own_part[:, TILE : 2 * TILE], 0).astype(BF16)
    chan[0:TILE, :] = jnp.where(later, 0, own_chan[length - TILE :, :]).astype(BF16)
    chan[TILE + length :, :] = jnp.where(later, own_chan[0:TILE, :], 0).astype(BF16)
    for copy in copies:
        copy.wait()
    correlate_all(part, chan, total, (a, b, c), 0, length + TILE, chunk, rows)
    total[...] = total[...] * scale


def split_second(chunk, scale, info, own_part, low_part, high_part, own_chan, chan_hbm, before, *rest):
    second_kernel(chunk, scale, info, own_part, (low_part, high_part), own_chan, chan_hbm, before, *rest)


def whole_kernel(chunk, scale, part_in, chan_in, total, part, chan, a, b, c):
    length = chan_in.shape[0]
    rows = part.shape[0]
    part[:, 0:TILE] = jnp.zeros((rows, TILE), BF16)
    part[:, TILE + length :] = jnp.zeros((rows, TILE), BF16)
    part[:, TILE : TILE + length] = part_in[...]
    edge = jnp.zeros((TILE, chan.shape[1]), BF16)
    chan[0:TILE, :] = edge
    chan[TILE + length :, :] = edge
    chan[TILE : TILE + length, :] = chan_in[...]
    total[...] = jnp.zeros_like(total)
    correlate_all(part, chan, total, (a, b, c), 0, length + TILE, chunk, rows)
    total[...] = total[...] * scale


def spare(rows, chunk):
    return [pltpu.VMEM((rows * (FINE + 1), width), BF16) for width in (chunk, chunk, TILE)]


def shifted(array, axis, step):
    count = lax.axis_size(axis)
    return lax.ppermute(array, axis, [(i, (i + step) % count) for i in range(count)])


def on_device(traces, filters, sources):
    chans, length = traces.shape
    partners = sources.shape[0]
    time_devs, chan_devs, sub_devs = (lax.axis_size(axis) for axis in ("tm", "chan", "sub"))
    here_tm, here_chan, here_sub = (lax.axis_index(axis) for axis in ("tm", "chan", "sub"))
    slots = min(chans, MOST)
    rows = partners // time_devs
    few = rows // sub_devs
    scale = 1.0 / math.sqrt(length * time_devs)
    chunk = 4 * TILE
    info = jnp.stack(
        [
            here_chan * sub_devs + here_sub,
            (here_tm > 0).astype(jnp.int32),
            (here_tm < time_devs - 1).astype(jnp.int32),
            here_chan,
            here_sub,
            here_tm,
            here_sub * few,
            (1 - here_sub) * few,
        ]
    ).astype(jnp.int32)
    taps = filters.T
    ring = time_devs == 2 and sub_devs == 2 and chan_devs <= 4
    flops = 2 * rows * LAGS * chans * length
    out_shape = jax.ShapeDtypeStruct((LAGS * rows, chans), F32)
    if ring:
        edge = lax.dynamic_slice_in_dim(traces, jnp.where(here_tm == 0, length - TILE, 0), TILE, 1)
        low = high = shifted(edge, "tm", 1)
    else:
        low = lax.ppermute(traces[:, length - TILE :], "tm", [(i, i + 1) for i in range(time_devs - 1)])
        high = lax.ppermute(traces[:, :TILE], "tm", [(i + 1, i) for i in range(time_devs - 1)])
    picked = whiten_slots(sources, info, traces, low, high, taps, slots)
    whitened = whiten(info, traces, low, high, taps)
    sizes = (chan_devs, sub_devs)
    if ring:
        near = [picked] + [shifted(picked, "chan", step) for step in range(1, chan_devs)]
        far = [shifted(part, "sub", 1) for part in near]
        own_part, send = order(info, sources, near + far, chans, sizes, True)
        other_chan = shifted(whitened, "tm", 1)
        low_part = shifted(send, "tm", 1)
        high_part = shifted(low_part, "sub", 1)
        before = pl.pallas_call(
            functools.partial(first_kernel, chunk),
            out_shape=out_shape,
            in_specs=[SMEM] + vmem(1) + [ANY],
            out_specs=vmem(1)[0],
            scratch_shapes=[pltpu.VMEM((length + 2 * TILE, chans), BF16)]
            + spare(rows, chunk)
            + [pltpu.SemaphoreType.DMA],
            compiler_params=params(),
            cost_estimate=cost(flops, 8 * rows * LAGS * chans),
            name="correlate_own",
        )(info, own_part, whitened)
        total = pl.pallas_call(
            functools.partial(split_second, chunk, scale),
            out_shape=out_shape,
            in_specs=[SMEM] + vmem(1) + [ANY, ANY] + vmem(1) + [ANY, ANY],
            out_specs=vmem(1)[0],
            scratch_shapes=[
                pltpu.VMEM((rows, length + 2 * TILE), BF16),
                pltpu.VMEM((length + 2 * TILE, chans), BF16),
            ]
            + spare(rows, chunk)
            + [pltpu.SemaphoreType.DMA((4,))],
            compiler_params=params(),
            cost_estimate=cost(flops, 8 * rows * LAGS * chans),
            name="correlate_other",
        )(info, own_part, low_part, high_part, whitened, other_chan, before)
    else:
        gathered = lax.all_gather(picked, ("chan", "sub"), axis=0, tiled=True)
        all_parts = order(info, sources, [gathered], chans, sizes, False)
        parts = lax.all_to_all(all_parts, "tm", 0, 1, tiled=True)
        all_chans = lax.all_gather(whitened, "tm", axis=0, tiled=True)
        full = length * time_devs
        total = pl.pallas_call(
            functools.partial(whole_kernel, chunk, scale),
            out_shape=out_shape,
            in_specs=vmem(2),
            out_specs=vmem(1)[0],
            scratch_shapes=[
                pltpu.VMEM((rows, full + 2 * TILE), BF16),
                pltpu.VMEM((full + 2 * TILE, chans), BF16),
            ]
            + spare(rows, chunk),
            compiler_params=params(),
            name="correlate_whole",
        )(parts, all_chans)
    return jnp.transpose(total.reshape(LAGS, rows, chans), (1, 0, 2))


def solution(mesh):
    return jax.shard_map(
        on_device,
        mesh=mesh,
        in_specs=(
            P(("groups", "chan", "sub"), "tm"),
            P(("groups", "chan", "sub"), None),
            P("groups"),
        ),
        out_specs=P("tm", None, ("groups", "chan", "sub")),
        check_vma=False,
    )
```

```python
import functools
import math

import jax
import jax.numpy as jnp
from jax import lax
from jax.experimental import pallas as pl
from jax.experimental.pallas import tpu as pltpu
from jax.sharding import PartitionSpec as P

LAGS = 129
MOST = 16
TILE = 128
FINE = 16
SETS = 24
F32 = jnp.float32
BF16 = jnp.bfloat16
VMEM_BYTES = 24 * 2**20


def vmem(count):
    return [pl.BlockSpec(memory_space=pltpu.VMEM)] * count


SMEM = pl.BlockSpec(memory_space=pltpu.SMEM)
ANY = pl.BlockSpec(memory_space=pl.ANY)


def params():
    return pltpu.CompilerParams(vmem_limit_bytes=VMEM_BYTES)


def light():
    return pl.CostEstimate(flops=1000, bytes_accessed=1000, transcendentals=0)


def set_sizes(taps):
    sizes = []
    for group in ((taps + 1) // 2, taps // 2, (taps + 1) // 2):
        sizes += [(group + 1) // 2, group // 2, (group + 1) // 2]
    return sizes


def split_taps(filters, sets, taps):
    def take(rows):
        return [filters[k : k + 1, :] if k < taps else None for k in rows]

    def plus(a, b):
        return [x if y is None else (y if x is None else x + y) for x, y in zip(a, b)]

    whole = 2 * ((taps + 1) // 2)
    even, odd = take(range(0, whole, 2)), take(range(1, whole, 2))
    for i, group in enumerate((even, odd, plus(even, odd))):
        group = group + [None] * (len(group) % 2)
        first, second = group[0::2], group[1::2]
        for j, rows in enumerate((first, second, plus(first, second))):
            for k, row in enumerate(rows):
                if row is not None:
                    at = SETS * (3 * i + j) + k
                    sets[at : at + 1, :] = row


def part_fir(stage, at, sets, row, count, rows):
    total = None
    for first in range(8):
        later = [j for j in range((count + 7) // 8) if first + 8 * j < count]
        window = stage[at + first : at + first + rows + 8 * later[-1], :]
        for j in later:
            k = row + first + 8 * j
            term = sets[k : k + 1, :] * window[8 * j : 8 * j + rows]
            total = term if total is None else total + term
    return total


def fir(samples, sets, stage, late, mixed, base, rows, counts):
    few = rows // 4
    extent = few + 32
    x3, x4, x5, x6 = (samples[pl.ds(base - 32 + p, extent, stride=4), :] for p in (3, 4, 5, 6))
    arrays = (x6, x4, x6 + x4, x5, x3, x5 + x3, x6 + x5, x4 + x3, (x6 + x4) + (x5 + x3))
    for i, array in enumerate(arrays):
        stage[i * extent : (i + 1) * extent, :] = array

    def halves(i, lead):
        size = few + lead
        at = 3 * i * extent
        p0 = part_fir(stage, at, sets, SETS * 3 * i, counts[3 * i], few + 8)
        p1 = part_fir(stage, at + extent + 8 - lead, sets, SETS * (3 * i + 1), counts[3 * i + 1], size)
        p2 = part_fir(stage, at + 2 * extent + 8 - lead, sets, SETS * (3 * i + 2), counts[3 * i + 2], size)
        late[8 : 16 + few, :] = p0
        return late[15 - lead : 15 - lead + size, :] + p1, p2 - p1 - late[16 - lead : 16 - lead + size, :]

    a_even, a_odd = halves(0, 8)
    b_even, b_odd = halves(1, 0)
    c_even, c_odd = halves(2, 0)
    mixed[0 : few + 8, :] = a_odd
    y0 = mixed[7 : 7 + few, :] + b_even
    y1 = c_even - a_even[8:] - b_even
    y2 = a_even[8:] + b_odd
    y3 = c_odd - a_odd[8:] - b_odd
    for p, y in enumerate((y0, y1, y2, y3)):
        mixed[pl.ds(p, few, stride=4), :] = y
    return mixed[0:rows, :]


def fir_scratch(rows, lanes):
    few = rows // 4
    return [
        pltpu.VMEM((9 * (few + 32), lanes), F32),
        pltpu.VMEM((few + 16, lanes), F32),
        pltpu.VMEM((max(rows, few + 8), lanes), F32),
    ]


def place_of(axes, sizes):
    at = 0
    for axis, size in zip(axes, sizes):
        at = at * size + lax.axis_index(axis)
    return at


def prepare_kernel(sizes, chans, ring, slots, sources, sources_row, filters, _, rows, sets, chan_taps, wanted, same):
    taps = filters.shape[0]
    first_chan = place_of(("chan", "sub"), sizes[1:]) * chans
    for s in range(slots):
        rows[s] = 0

    def find(p, count):
        local = sources[p] - first_chan
        mine = (local >= 0) & (local < chans)
        rows[jnp.where(mine, count, slots)] = local
        return count + mine.astype(jnp.int32)

    lax.fori_loop(0, sources.shape[0], find, 0, unroll=16)
    split_taps(filters, sets, taps)
    chan_taps[...] = jnp.concatenate([filters[...], jnp.zeros((TILE - taps, chans), F32)], 0).T
    partners = sources_row.shape[1]
    _, chan_devs, sub_devs = sizes
    own_row = jnp.broadcast_to(sources_row[...].astype(F32), (partners, partners))
    owner_row = jnp.floor((own_row + 0.5) * (1.0 / chans))
    owner_col = owner_row.T
    lane = lax.broadcasted_iota(jnp.int32, (partners, partners), 1)
    line = lax.broadcasted_iota(jnp.int32, (partners, partners), 0)
    earlier = (owner_row == owner_col) & (lane < line)
    rank = jnp.sum(earlier.astype(F32), axis=1, keepdims=True)
    owner = owner_col[:, 0:1]
    if ring:
        owner_chan = jnp.floor((owner + 0.5) * (1.0 / sub_devs))
        owner_sub = owner - sub_devs * owner_chan
        my_chan = lax.axis_index("chan").astype(F32)
        my_sub = lax.axis_index("sub").astype(F32)
        behind = my_chan - owner_chan
        behind = jnp.where(behind < 0, behind + chan_devs, behind)
        place = jnp.where(owner_sub == my_sub, 0.0, 1.0) * chan_devs + behind
    else:
        place = owner
    at = lax.broadcasted_iota(jnp.int32, wanted.shape, 1).astype(F32)
    wanted[...] = (place * slots + rank == at).astype(F32)


def prepare(sizes, sources, filters, traces, slots, ring):
    taps, chans = filters.shape
    partners = sources.shape[0]
    total = slots * sizes[1] * sizes[2]
    return pl.pallas_call(
        functools.partial(prepare_kernel, sizes, chans, ring, slots),
        out_shape=(
            jax.ShapeDtypeStruct((slots + 1,), jnp.int32),
            jax.ShapeDtypeStruct((9 * SETS, chans), F32),
            jax.ShapeDtypeStruct((chans, TILE), F32),
            jax.ShapeDtypeStruct((partners, total), F32),
            jax.ShapeDtypeStruct(traces.shape, F32),
        ),
        in_specs=[SMEM] + vmem(2) + [ANY],
        out_specs=(SMEM, *vmem(3), ANY),
        input_output_aliases={3: 4},
        compiler_params=params(),
        cost_estimate=light(),
        name="prepare",
    )(sources, sources.reshape(1, partners), filters, traces)


def slots_kernel(taps, sizes, rows, x, low, high, chan_taps, after, out, wide, tall, lane_taps, *work):
    chans, length = x.shape
    slots = out.shape[0]
    segs = TILE // slots
    seg_len = length // segs
    half = (taps - 1) // 2
    here = lax.axis_index("tm")
    keep_low = (here > 0).astype(F32)
    keep_high = (here < sizes[0] - 1).astype(F32)
    for s in range(slots):
        row = rows[s]
        group = pl.multiple_of((row >> 3) << 3, 8)
        turn = (s - row) & 7

        def pick(ref):
            return pltpu.roll(ref[pl.ds(group, 8), :], turn, 0)[s % 8 : s % 8 + 1, :]

        wide[s : s + 1, 0:TILE] = pick(low) * keep_low
        wide[s : s + 1, TILE : TILE + length] = pick(x)
        wide[s : s + 1, TILE + length :] = pick(high) * keep_high
        lane_taps[s : s + 1, :] = pick(chan_taps)
    picked = lane_taps[0:slots, :]
    lane_taps[...] = jnp.concatenate([picked] * segs, 0).T
    for t in range(seg_len // TILE + 2):
        cols = [wide[:, g * seg_len + t * TILE : g * seg_len + (t + 1) * TILE] for g in range(segs)]
        tall[t * TILE : (t + 1) * TILE, :] = jnp.concatenate(cols, 0).T
    split_taps(lane_taps, work[0], taps)
    counts = set_sizes(taps)
    done = fir(tall, *work, TILE - half, seg_len, counts)
    for t in range(seg_len // TILE):
        turned = done[t * TILE : (t + 1) * TILE].T
        for g in range(segs):
            start = g * seg_len + t * TILE
            out[:, start : start + TILE] = turned[g * slots : (g + 1) * slots].astype(BF16)


def whiten_slots(sizes, taps, rows, traces, low, high, chan_taps, after, slots):
    length = traces.shape[1]
    seg_len = length * slots // TILE
    return pl.pallas_call(
        functools.partial(slots_kernel, taps, sizes),
        out_shape=jax.ShapeDtypeStruct((slots, length), BF16),
        in_specs=[SMEM] + vmem(4) + [ANY],
        out_specs=vmem(1)[0],
        scratch_shapes=[
            pltpu.VMEM((slots, length + 2 * TILE), F32),
            pltpu.VMEM((seg_len + 2 * TILE, TILE), F32),
            pltpu.VMEM((TILE, TILE), F32),
        ]
        + [pltpu.VMEM((9 * SETS, TILE), F32)]
        + fir_scratch(seg_len, TILE),
        compiler_params=params(),
        cost_estimate=light(),
        name="whiten_slots",
    )(rows, traces, low, high, chan_taps, after)


def whiten_kernel(taps, rows, time_devs, x, low, high, sets, out, tall, *work):
    length = x.shape[1]
    half = (taps - 1) // 2
    here = lax.axis_index("tm")
    tall[0:TILE, :] = jnp.where(here > 0, low[...], 0.0).T
    tall[TILE + length :, :] = jnp.where(here < time_devs - 1, high[...], 0.0).T
    counts = set_sizes(taps)

    def turn(t, carry):
        start = pl.multiple_of(t * TILE, TILE)
        tall[pl.ds(start + TILE, TILE), :] = x[:, pl.ds(start, TILE)].T
        return carry

    lax.fori_loop(0, length // TILE, turn, 0)

    def block(i, carry):
        at = pl.multiple_of(i * rows, rows)
        out[pl.ds(at, rows), :] = fir(tall, sets, *work, at + TILE - half, rows, counts).astype(BF16)
        return carry

    lax.fori_loop(0, length // rows, block, 0)


def whiten(time_devs, taps, traces, low, high, sets):
    chans, length = traces.shape
    rows = 2 * TILE
    return pl.pallas_call(
        functools.partial(whiten_kernel, taps, rows, time_devs),
        out_shape=jax.ShapeDtypeStruct((length, chans), BF16),
        in_specs=vmem(4),
        out_specs=vmem(1)[0],
        scratch_shapes=[pltpu.VMEM((length + 2 * TILE, chans), F32)] + fir_scratch(rows, chans),
        compiler_params=params(),
        cost_estimate=light(),
        name="whiten",
    )(traces, low, high, sets)


def whiten_part_kernel(taps, rows, inner, x, sets, beside, _, *refs):
    outs, (tall, *work) = refs[:-4], refs[-4:]
    length, size = x.shape[1], tall.shape[0] - 2 * TILE
    half = (taps - 1) // 2
    tiles = rows // TILE
    at_start = (lax.axis_index("tm") > 0) == inner
    start = jnp.where(at_start, 0, length - size)
    near = x[:, pl.ds(pl.multiple_of(jnp.where(at_start, size, length - size - TILE), TILE), TILE)]
    outside = beside[...] if inner else jnp.zeros_like(near)
    tall[0:TILE, :] = jnp.where(at_start, outside, near).T
    tall[TILE + size :, :] = jnp.where(at_start, near, outside).T
    counts = set_sizes(taps)

    def turn(t):
        tall[pl.ds(pl.multiple_of(t * TILE + TILE, TILE), TILE), :] = x[
            :, pl.ds(pl.multiple_of(start + t * TILE, TILE), TILE)
        ].T

    for t in range(tiles + 1):
        turn(t)

    done = 0
    for out in outs:

        def block(i, carry):
            at = pl.multiple_of(i * rows, rows)
            value = fir(tall, sets, *work, at + TILE - half, rows, counts).astype(BF16)
            out[pl.ds(at - done, rows), :] = value
            for t in range(tiles):
                turn(jnp.minimum((i + 1) * tiles + 1 + t, size // TILE - 1))
            return carry

        lax.fori_loop(done // rows, (done + out.shape[0]) // rows, block, 0)
        done += out.shape[0]


def whiten_part(taps, traces, sets, beside, after, pieces, inner):
    chans = traces.shape[0]
    size = sum(pieces)
    rows = 2 * TILE
    return pl.pallas_call(
        functools.partial(whiten_part_kernel, taps, rows, inner),
        out_shape=tuple(jax.ShapeDtypeStruct((piece, chans), BF16) for piece in pieces),
        in_specs=vmem(3) + [ANY],
        out_specs=tuple(vmem(len(pieces))),
        scratch_shapes=[pltpu.VMEM((size + 2 * TILE, chans), F32)] + fir_scratch(rows, chans),
        compiler_params=params(),
        cost_estimate=light(),
        name="whiten_inner" if inner else "whiten_outer",
    )(traces, sets, beside, after)


def join_kernel(parts, count, after, *refs):
    size = refs[0].shape[0]
    each = count // parts
    for n in range(parts):
        for i in range(each):
            refs[count + n][i * size : (i + 1) * size, :] = refs[n * each + i][...]


def join(after, parts, pieces):
    size, length = parts[0].shape
    shape = jax.ShapeDtypeStruct((size * len(parts) // pieces, length), BF16)
    return pl.pallas_call(
        functools.partial(join_kernel, pieces, len(parts)),
        out_shape=(shape,) * pieces,
        in_specs=[ANY] + vmem(len(parts)),
        out_specs=tuple(vmem(pieces)),
        compiler_params=params(),
        cost_estimate=light(),
        name="join_slots",
    )(after, *parts)


def order_kernel(ring, count, choose, after, *refs):
    parts, (*outs, gathered) = refs[:count], refs[count:]
    step = parts[0].shape[0]
    for i, part in enumerate(parts):
        gathered[i * step : (i + 1) * step, :] = part[...]
    if not ring:
        outs[0][...] = jnp.dot(choose[...].astype(BF16), gathered[...], preferred_element_type=F32).astype(BF16)
        return
    own, send = outs
    half, length = send.shape
    here = lax.axis_index("tm")
    mine = choose[pl.ds(pl.multiple_of(here * half, half), half), :]
    theirs = choose[pl.ds(pl.multiple_of((1 - here) * half, half), half), :]
    wanted = jnp.concatenate([mine, theirs], 0).astype(BF16)
    got = jnp.dot(wanted, gathered[...], preferred_element_type=F32).astype(BF16)
    own[:, 0:TILE] = jnp.zeros((half, TILE), BF16)
    own[:, TILE + length :] = jnp.zeros((half, TILE), BF16)
    own[:, TILE : TILE + length] = got[:half]
    send[...] = got[half:]


def order(choose, after, parts, ring):
    partners, total = choose.shape
    length = parts[0].shape[1]
    if ring:
        half = partners // 2
        out_shape = (
            jax.ShapeDtypeStruct((half, length + 2 * TILE), BF16),
            jax.ShapeDtypeStruct((half, length), BF16),
        )
        out_specs = tuple(vmem(2))
    else:
        out_shape = jax.ShapeDtypeStruct((partners, length), BF16)
        out_specs = vmem(1)[0]
    return pl.pallas_call(
        functools.partial(order_kernel, ring, len(parts)),
        out_shape=out_shape,
        in_specs=vmem(1) + [ANY] + vmem(len(parts)),
        out_specs=out_specs,
        scratch_shapes=[pltpu.VMEM((total, length), BF16)],
        compiler_params=params(),
        cost_estimate=light(),
        name="order_partners",
    )(choose, after, *parts)


def lay_out(part, out, start, width):
    rows = part.shape[0]
    lane = lax.broadcasted_iota(jnp.int32, (rows, TILE), 1)
    tiles = [part[:, pl.ds(start + TILE * i, TILE)] for i in range(width // TILE + 1)]
    half = (LAGS - 1) // 2
    for b in range(FINE + 1):
        turned = [pltpu.roll(tile, half - b, 1) for tile in tiles]
        for i in range(width // TILE):
            piece = jnp.where(lane < half - b, turned[i], turned[i + 1])
            out[b * rows : (b + 1) * rows, TILE * i : TILE * i + TILE] = piece


def add_lags(shifted, chan, total, start, width, rows):
    chans = chan.shape[1]
    coarse = (LAGS - 1) // FINE
    pair = 2 if chans % TILE == 0 else 1
    for a in range(0, coarse, pair):
        cols = [chan[pl.ds(start + TILE - FINE * (a + i), width), :] for i in range(pair)]
        last = a + pair == coarse
        used = rows * (FINE + 1 if last else FINE)
        block = cols[0] if pair == 1 else jnp.concatenate(cols, 1)
        term = jnp.dot(shifted[:used, :], block, preferred_element_type=F32)
        for i in range(pair):
            size = used if i == pair - 1 else rows * FINE
            place = (a + i) * FINE * rows
            total[place : place + size, :] += term[:size, i * chans : (i + 1) * chans]


def correlate_all(part, chan, total, spare, start, width, chunk, rows):
    first, second, rest = spare
    whole = width // (2 * chunk) * (2 * chunk)
    lay_out(part, first, start, chunk)

    def advance(i, carry):
        now = pl.multiple_of(start + 2 * chunk * i, TILE)
        lay_out(part, second, now + chunk, chunk)
        add_lags(first, chan, total, now, chunk, rows)
        after = pl.multiple_of(jnp.minimum(now + 2 * chunk, start + whole - chunk), TILE)
        lay_out(part, first, after, chunk)
        add_lags(second, chan, total, now + chunk, chunk, rows)
        return carry

    lax.fori_loop(0, whole // (2 * chunk), advance, 0)
    if width > whole:
        lay_out(part, rest, start + whole, width - whole)
        add_lags(rest, chan, total, start + whole, width - whole, rows)


def add_pair(shifted, chan, before, total, start, width, rows, a, scale):
    chans = chan.shape[1]
    last = a + 2 == (LAGS - 1) // FINE
    used = rows * (FINE + 1 if last else FINE)
    term = None
    for copies, begin in zip(shifted, start):
        cols = [chan[pl.ds(begin + TILE - FINE * (a + i), width), :] for i in range(2)]
        piece = jnp.dot(copies[:used, :], jnp.concatenate(cols, 1), preferred_element_type=F32)
        term = piece if term is None else term + piece
    for i in range(2):
        size = used if i == 1 else rows * FINE
        place = (a + i) * FINE * rows
        mine = term[:size, i * chans : (i + 1) * chans]
        if before is not None:
            mine = before[place : place + size, :] + mine
        total[place : place + size, :] = mine if scale is None else mine * scale


def correlate_ring(part, chan, total, spare, start, width, chunk, rows, ready, before, scale, out, sems):
    pairs = range(0, (LAGS - 1) // FINE, 2)
    rest = width % chunk
    count = width // chunk
    begin = [pl.multiple_of(start + rest + i * chunk, TILE) for i in range(count)]
    if rest:
        lay_out(part, spare[3], start, rest)
    lay_out(part, spare[0], begin[0], chunk)
    for copy in ready:
        copy.wait()
    if rest:
        for a in pairs:
            add_pair([spare[3]], chan, before, total, [start], rest, rows, a, None)
        before = total
    for i in range(count - 2):
        lay_out(part, spare[(i + 1) % 3], begin[i + 1], chunk)
        if i == count - 3:
            lay_out(part, spare[(i + 2) % 3], begin[i + 2], chunk)
        for a in pairs:
            add_pair([spare[i % 3]], chan, before, total, [begin[i]], chunk, rows, a, None)
        before = total
    stores = []
    for n, a in enumerate(pairs):
        ends = (count - 2, count - 1)
        add_pair([spare[i % 3] for i in ends], chan, before, total, [begin[i] for i in ends], chunk, rows, a, scale)
        if out is not None:
            at = 2 * n * FINE * rows
            size = rows * (2 * FINE + (1 if a + 2 == (LAGS - 1) // FINE else 0))
            stores.append(pltpu.make_async_copy(total.at[pl.ds(at, size), :], out.at[pl.ds(at, size), :], sems.at[n]))
            stores[-1].start()
    for store in stores:
        store.wait()


def place_pieces(at_start, pieces, chan, length, sems):
    outer = pieces[0].shape[0]
    at = jnp.where(at_start, 0, length - outer)
    copies = []
    for n, piece in enumerate(pieces):
        size = piece.shape[0]
        to = chan.at[pl.ds(pl.multiple_of(TILE + at, TILE), size), :]
        copies.append(pltpu.make_async_copy(piece, to, sems.at[4 + n]))
        copies[-1].start()
        at = jnp.where(at_start, outer, 0) if n == 0 else at + size
    return copies


def first_kernel(chunk, count, part, *refs):
    pieces, (total, chan, a, b, c, d, sems) = refs[:count], refs[count:]
    length = part.shape[1] - 2 * TILE
    here = lax.axis_index("tm")
    ready = place_pieces(here == 0, pieces, chan, length, sems)
    edge = jnp.zeros((TILE, chan.shape[1]), BF16)
    chan[0:TILE, :] = edge
    chan[TILE + length :, :] = edge
    start = pl.multiple_of(here * TILE, TILE)
    correlate_ring(part, chan, total, (a, b, c, d), start, length, chunk, part.shape[0], ready, None, None, None, sems)


def second_kernel(chunk, scale, count, own_part, other_part, own_head, own_tail, before, *refs):
    pieces, (out, total, part, chan, a, b, c, d, sems) = refs[:count], refs[count:]
    length = part.shape[1] - 2 * TILE
    rows = part.shape[0]
    here = lax.axis_index("tm")
    ready = place_pieces(here > 0, pieces, chan, length, sems)
    later = here > 0
    part[:, TILE : TILE + length] = other_part[...]
    part[:, 0:TILE] = jnp.where(later, 0, own_part[:, length : length + TILE]).astype(BF16)
    part[:, TILE + length :] = jnp.where(later, own_part[:, TILE : 2 * TILE], 0).astype(BF16)
    chan[0:TILE, :] = jnp.where(later, 0, own_tail[own_tail.shape[0] - TILE :, :]).astype(BF16)
    chan[TILE + length :, :] = jnp.where(later, own_head[0:TILE, :], 0).astype(BF16)
    correlate_ring(part, chan, total, (a, b, c, d), 0, length + TILE, chunk, rows, ready, before, scale, out, sems)


def whole_kernel(chunk, scale, part_in, chan_in, total, part, chan, a, b, c):
    length = chan_in.shape[0]
    rows = part.shape[0]
    part[:, 0:TILE] = jnp.zeros((rows, TILE), BF16)
    part[:, TILE + length :] = jnp.zeros((rows, TILE), BF16)
    part[:, TILE : TILE + length] = part_in[...]
    edge = jnp.zeros((TILE, chan.shape[1]), BF16)
    chan[0:TILE, :] = edge
    chan[TILE + length :, :] = edge
    chan[TILE : TILE + length, :] = chan_in[...]
    total[...] = jnp.zeros_like(total)
    correlate_all(part, chan, total, (a, b, c), 0, length + TILE, chunk, rows)
    total[...] = total[...] * scale


def spare(rows, widths):
    return [pltpu.VMEM((rows * (FINE + 1), width), BF16) for width in widths]


def shifted(array, axis, step):
    count = lax.axis_size(axis)
    return lax.ppermute(array, axis, [(i, (i + step) % count) for i in range(count)])


def on_device(traces, filters, sources):
    chans, length = traces.shape
    partners = sources.shape[0]
    sizes = tuple(lax.axis_size(axis) for axis in ("tm", "chan", "sub"))
    time_devs, chan_devs, sub_devs = sizes
    slots = min(chans, MOST)
    rows = partners // time_devs
    scale = 1.0 / math.sqrt(length * time_devs)
    chunk = 4 * TILE
    taps = filters.T
    ring = time_devs == 2 and sub_devs == 2 and chan_devs <= 4 and chans % TILE == 0
    out_shape = jax.ShapeDtypeStruct((LAGS * rows, chans), F32)
    count = taps.shape[0]
    slot_rows, sets, chan_taps, choose, held = prepare(sizes, sources, taps, traces, slots, ring)
    if ring:
        here = lax.axis_index("tm")
        edge = lax.dynamic_slice_in_dim(traces, jnp.where(here == 0, length - TILE, 0), TILE, 1)
        beside = shifted(edge, "tm", 1)
        far = length // 2
        outer = whiten_part(count, held, sets, beside, beside, (length // 2,), False)
        other_outer = [shifted(piece, "tm", 1) for piece in outer]
        picked = whiten_slots(sizes, count, slot_rows, held, beside, beside, chan_taps, outer[0], slots)
        inner = whiten_part(count, held, sets, beside, picked, (length // 2,), True)
        other_inner = [shifted(piece, "tm", 1) for piece in inner]
        near = [picked] + [shifted(picked, "chan", step) for step in range(1, chan_devs)]
        mine = join(other_outer[0], near, 1)
        theirs = [shifted(part, "sub", 1) for part in mine]
        own_part, send = order(choose, other_inner[0], [*mine, *theirs], True)
        other_part = shifted(send, "tm", 1)
        pieces = len(outer) + len(inner)
        before = pl.pallas_call(
            functools.partial(first_kernel, chunk, pieces),
            out_shape=out_shape,
            in_specs=vmem(1) + [ANY] * pieces,
            out_specs=vmem(1)[0],
            scratch_shapes=[pltpu.VMEM((length + 2 * TILE, chans), BF16)]
            + spare(rows, (chunk, chunk, chunk, TILE))
            + [pltpu.SemaphoreType.DMA((4 + pieces,))],
            compiler_params=params(),
            cost_estimate=light(),
            name="correlate_own",
        )(own_part, *outer, *inner)
        total = pl.pallas_call(
            functools.partial(second_kernel, chunk, scale, pieces),
            out_shape=out_shape,
            in_specs=vmem(5) + [ANY] * pieces,
            out_specs=ANY,
            scratch_shapes=[
                pltpu.VMEM(out_shape.shape, F32),
                pltpu.VMEM((rows, length + 2 * TILE), BF16),
                pltpu.VMEM((length + 2 * TILE, chans), BF16),
            ]
            + spare(rows, (chunk, chunk, chunk, TILE))
            + [pltpu.SemaphoreType.DMA((4 + pieces,))],
            compiler_params=params(),
            cost_estimate=light(),
            name="correlate_other",
        )(own_part, other_part, inner[0], inner[-1], before, *other_outer, *other_inner)
    else:
        low = lax.ppermute(traces[:, length - TILE :], "tm", [(i, i + 1) for i in range(time_devs - 1)])
        high = lax.ppermute(traces[:, :TILE], "tm", [(i + 1, i) for i in range(time_devs - 1)])
        picked = whiten_slots(sizes, count, slot_rows, held, low, high, chan_taps, low, slots)
        whitened = whiten(time_devs, count, traces, low, high, sets)
        gathered = lax.all_gather(picked, ("chan", "sub"), axis=0, tiled=True)
        all_parts = order(choose, low, [gathered], False)
        parts = lax.all_to_all(all_parts, "tm", 0, 1, tiled=True)
        all_chans = lax.all_gather(whitened, "tm", axis=0, tiled=True)
        full = length * time_devs
        total = pl.pallas_call(
            functools.partial(whole_kernel, chunk, scale),
            out_shape=out_shape,
            in_specs=vmem(2),
            out_specs=vmem(1)[0],
            scratch_shapes=[
                pltpu.VMEM((rows, full + 2 * TILE), BF16),
                pltpu.VMEM((full + 2 * TILE, chans), BF16),
            ]
            + spare(rows, (chunk, chunk, TILE)),
            compiler_params=pltpu.CompilerParams(vmem_limit_bytes=2 * VMEM_BYTES),
            name="correlate_whole",
        )(parts, all_chans)
    return jnp.transpose(total.reshape(LAGS, rows, chans), (1, 0, 2))


def solution(mesh):
    return jax.shard_map(
        on_device,
        mesh=mesh,
        in_specs=(
            P(("groups", "chan", "sub"), "tm"),
            P(("groups", "chan", "sub"), None),
            P("groups"),
        ),
        out_specs=P("tm", None, ("groups", "chan", "sub")),
        check_vma=False,
    )
```

```python
import functools
import math

import jax
import jax.numpy as jnp
from jax import lax
from jax.experimental import pallas as pl
from jax.experimental.pallas import tpu as pltpu
from jax.sharding import PartitionSpec as P

LAGS = 129
MOST = 16
TILE = 128
FINE = 16
SETS = 24
ARRIVED = 2
F32 = jnp.float32
BF16 = jnp.bfloat16
VMEM_BYTES = 24 * 2**20


def vmem(count):
    return [pl.BlockSpec(memory_space=pltpu.VMEM)] * count


SMEM = pl.BlockSpec(memory_space=pltpu.SMEM)
ANY = pl.BlockSpec(memory_space=pl.ANY)


def params():
    return pltpu.CompilerParams(vmem_limit_bytes=VMEM_BYTES)


def light():
    return pl.CostEstimate(flops=1000, bytes_accessed=1000, transcendentals=0)


def set_sizes(taps):
    sizes = []
    for group in ((taps + 1) // 2, taps // 2, (taps + 1) // 2):
        sizes += [(group + 1) // 2, group // 2, (group + 1) // 2]
    return sizes


def split_taps(filters, sets, taps):
    def take(rows):
        return [filters[k : k + 1, :] if k < taps else None for k in rows]

    def plus(a, b):
        return [x if y is None else (y if x is None else x + y) for x, y in zip(a, b)]

    whole = 2 * ((taps + 1) // 2)
    even, odd = take(range(0, whole, 2)), take(range(1, whole, 2))
    for i, group in enumerate((even, odd, plus(even, odd))):
        group = group + [None] * (len(group) % 2)
        first, second = group[0::2], group[1::2]
        for j, rows in enumerate((first, second, plus(first, second))):
            for k, row in enumerate(rows):
                if row is not None:
                    at = SETS * (3 * i + j) + k
                    sets[at : at + 1, :] = row


def part_fir(stage, at, sets, row, count, rows):
    total = None
    for first in range(8):
        later = [j for j in range((count + 7) // 8) if first + 8 * j < count]
        window = stage[at + first : at + first + rows + 8 * later[-1], :]
        for j in later:
            k = row + first + 8 * j
            term = sets[k : k + 1, :] * window[8 * j : 8 * j + rows]
            total = term if total is None else total + term
    return total


def fir(samples, sets, stage, late, mixed, base, rows, counts):
    few = rows // 4
    extent = few + 32
    x3, x4, x5, x6 = (samples[pl.ds(base - 32 + p, extent, stride=4), :] for p in (3, 4, 5, 6))
    arrays = (x6, x4, x6 + x4, x5, x3, x5 + x3, x6 + x5, x4 + x3, (x6 + x4) + (x5 + x3))
    for i, array in enumerate(arrays):
        stage[i * extent : (i + 1) * extent, :] = array

    def halves(i, lead):
        size = few + lead
        at = 3 * i * extent
        p0 = part_fir(stage, at, sets, SETS * 3 * i, counts[3 * i], few + 8)
        p1 = part_fir(stage, at + extent + 8 - lead, sets, SETS * (3 * i + 1), counts[3 * i + 1], size)
        p2 = part_fir(stage, at + 2 * extent + 8 - lead, sets, SETS * (3 * i + 2), counts[3 * i + 2], size)
        late[8 : 16 + few, :] = p0
        return late[15 - lead : 15 - lead + size, :] + p1, p2 - p1 - late[16 - lead : 16 - lead + size, :]

    a_even, a_odd = halves(0, 8)
    b_even, b_odd = halves(1, 0)
    c_even, c_odd = halves(2, 0)
    mixed[0 : few + 8, :] = a_odd
    y0 = mixed[7 : 7 + few, :] + b_even
    y1 = c_even - a_even[8:] - b_even
    y2 = a_even[8:] + b_odd
    y3 = c_odd - a_odd[8:] - b_odd
    for p, y in enumerate((y0, y1, y2, y3)):
        mixed[pl.ds(p, few, stride=4), :] = y
    return mixed[0:rows, :]


def fir_scratch(rows, lanes):
    few = rows // 4
    return [
        pltpu.VMEM((9 * (few + 32), lanes), F32),
        pltpu.VMEM((few + 16, lanes), F32),
        pltpu.VMEM((max(rows, few + 8), lanes), F32),
    ]


def place_of(axes, sizes):
    at = 0
    for axis, size in zip(axes, sizes):
        at = at * size + lax.axis_index(axis)
    return at


def prepare_kernel(sizes, chans, ring, slots, sources, sources_row, filters, _, rows, sets, chan_taps, wanted, same):
    taps = filters.shape[0]
    first_chan = place_of(("chan", "sub"), sizes[1:]) * chans
    for s in range(slots):
        rows[s] = 0

    def find(p, count):
        local = sources[p] - first_chan
        mine = (local >= 0) & (local < chans)
        rows[jnp.where(mine, count, slots)] = local
        return count + mine.astype(jnp.int32)

    lax.fori_loop(0, sources.shape[0], find, 0, unroll=16)
    split_taps(filters, sets, taps)
    chan_taps[...] = jnp.concatenate([filters[...], jnp.zeros((TILE - taps, chans), F32)], 0).T
    partners = sources_row.shape[1]
    _, chan_devs, sub_devs = sizes
    own_row = jnp.broadcast_to(sources_row[...].astype(F32), (partners, partners))
    owner_row = jnp.floor((own_row + 0.5) * (1.0 / chans))
    owner_col = owner_row.T
    lane = lax.broadcasted_iota(jnp.int32, (partners, partners), 1)
    line = lax.broadcasted_iota(jnp.int32, (partners, partners), 0)
    earlier = (owner_row == owner_col) & (lane < line)
    rank = jnp.sum(earlier.astype(F32), axis=1, keepdims=True)
    owner = owner_col[:, 0:1]
    if ring:
        owner_chan = jnp.floor((owner + 0.5) * (1.0 / sub_devs))
        owner_sub = owner - sub_devs * owner_chan
        my_chan = lax.axis_index("chan").astype(F32)
        my_sub = lax.axis_index("sub").astype(F32)
        behind = my_chan - owner_chan
        behind = jnp.where(behind < 0, behind + chan_devs, behind)
        place = jnp.where(owner_sub == my_sub, 0.0, 1.0) * chan_devs + behind
    else:
        place = owner
    at = lax.broadcasted_iota(jnp.int32, wanted.shape, 1).astype(F32)
    wanted[...] = (place * slots + rank == at).astype(F32)


def prepare(sizes, sources, filters, traces, slots, ring):
    taps, chans = filters.shape
    partners = sources.shape[0]
    total = slots * sizes[1] * sizes[2]
    return pl.pallas_call(
        functools.partial(prepare_kernel, sizes, chans, ring, slots),
        out_shape=(
            jax.ShapeDtypeStruct((slots + 1,), jnp.int32),
            jax.ShapeDtypeStruct((9 * SETS, chans), F32),
            jax.ShapeDtypeStruct((chans, TILE), F32),
            jax.ShapeDtypeStruct((partners, total), F32),
            jax.ShapeDtypeStruct(traces.shape, F32),
        ),
        in_specs=[SMEM] + vmem(2) + [ANY],
        out_specs=(SMEM, *vmem(3), ANY),
        input_output_aliases={3: 4},
        compiler_params=params(),
        cost_estimate=light(),
        name="prepare",
    )(sources, sources.reshape(1, partners), filters, traces)


def slots_kernel(taps, sizes, rows, x, low, high, chan_taps, after, out, wide, tall, lane_taps, *work):
    chans, length = x.shape
    slots = out.shape[0]
    segs = TILE // slots
    seg_len = length // segs
    half = (taps - 1) // 2
    here = lax.axis_index("tm")
    keep_low = (here > 0).astype(F32)
    keep_high = (here < sizes[0] - 1).astype(F32)
    for s in range(slots):
        row = rows[s]
        group = pl.multiple_of((row >> 3) << 3, 8)
        turn = (s - row) & 7

        def pick(ref):
            return pltpu.roll(ref[pl.ds(group, 8), :], turn, 0)[s % 8 : s % 8 + 1, :]

        wide[s : s + 1, 0:TILE] = pick(low) * keep_low
        wide[s : s + 1, TILE : TILE + length] = pick(x)
        wide[s : s + 1, TILE + length :] = pick(high) * keep_high
        lane_taps[s : s + 1, :] = pick(chan_taps)
    picked = lane_taps[0:slots, :]
    lane_taps[...] = jnp.concatenate([picked] * segs, 0).T
    for t in range(seg_len // TILE + 2):
        cols = [wide[:, g * seg_len + t * TILE : g * seg_len + (t + 1) * TILE] for g in range(segs)]
        tall[t * TILE : (t + 1) * TILE, :] = jnp.concatenate(cols, 0).T
    split_taps(lane_taps, work[0], taps)
    counts = set_sizes(taps)
    done = fir(tall, *work, TILE - half, seg_len, counts)
    for t in range(seg_len // TILE):
        turned = done[t * TILE : (t + 1) * TILE].T
        for g in range(segs):
            start = g * seg_len + t * TILE
            out[:, start : start + TILE] = turned[g * slots : (g + 1) * slots].astype(BF16)


def whiten_slots(sizes, taps, rows, traces, low, high, chan_taps, after, slots):
    length = traces.shape[1]
    seg_len = length * slots // TILE
    return pl.pallas_call(
        functools.partial(slots_kernel, taps, sizes),
        out_shape=jax.ShapeDtypeStruct((slots, length), BF16),
        in_specs=[SMEM] + vmem(4) + [ANY],
        out_specs=vmem(1)[0],
        scratch_shapes=[
            pltpu.VMEM((slots, length + 2 * TILE), F32),
            pltpu.VMEM((seg_len + 2 * TILE, TILE), F32),
            pltpu.VMEM((TILE, TILE), F32),
        ]
        + [pltpu.VMEM((9 * SETS, TILE), F32)]
        + fir_scratch(seg_len, TILE),
        compiler_params=params(),
        cost_estimate=light(),
        name="whiten_slots",
    )(rows, traces, low, high, chan_taps, after)


def whiten_kernel(taps, rows, time_devs, x, low, high, sets, out, tall, *work):
    length = x.shape[1]
    half = (taps - 1) // 2
    here = lax.axis_index("tm")
    tall[0:TILE, :] = jnp.where(here > 0, low[...], 0.0).T
    tall[TILE + length :, :] = jnp.where(here < time_devs - 1, high[...], 0.0).T
    counts = set_sizes(taps)

    def turn(t, carry):
        start = pl.multiple_of(t * TILE, TILE)
        tall[pl.ds(start + TILE, TILE), :] = x[:, pl.ds(start, TILE)].T
        return carry

    lax.fori_loop(0, length // TILE, turn, 0)

    def block(i, carry):
        at = pl.multiple_of(i * rows, rows)
        out[pl.ds(at, rows), :] = fir(tall, sets, *work, at + TILE - half, rows, counts).astype(BF16)
        return carry

    lax.fori_loop(0, length // rows, block, 0)


def whiten(time_devs, taps, traces, low, high, sets):
    chans, length = traces.shape
    rows = 2 * TILE
    return pl.pallas_call(
        functools.partial(whiten_kernel, taps, rows, time_devs),
        out_shape=jax.ShapeDtypeStruct((length, chans), BF16),
        in_specs=vmem(4),
        out_specs=vmem(1)[0],
        scratch_shapes=[pltpu.VMEM((length + 2 * TILE, chans), F32)] + fir_scratch(rows, chans),
        compiler_params=params(),
        cost_estimate=light(),
        name="whiten",
    )(traces, low, high, sets)


def whiten_part_kernel(taps, rows, inner, x, sets, beside, _, *refs):
    outs, (tall, *work) = refs[:-4], refs[-4:]
    length, size = x.shape[1], tall.shape[0] - 2 * TILE
    half = (taps - 1) // 2
    tiles = rows // TILE
    at_start = (lax.axis_index("tm") > 0) == inner
    start = jnp.where(at_start, 0, length - size)
    near = x[:, pl.ds(pl.multiple_of(jnp.where(at_start, size, length - size - TILE), TILE), TILE)]
    outside = beside[...] if inner else jnp.zeros_like(near)
    tall[0:TILE, :] = jnp.where(at_start, outside, near).T
    tall[TILE + size :, :] = jnp.where(at_start, near, outside).T
    counts = set_sizes(taps)

    def turn(t):
        tall[pl.ds(pl.multiple_of(t * TILE + TILE, TILE), TILE), :] = x[
            :, pl.ds(pl.multiple_of(start + t * TILE, TILE), TILE)
        ].T

    for t in range(tiles + 1):
        turn(t)

    done = 0
    for out in outs:

        def block(i, carry):
            at = pl.multiple_of(i * rows, rows)
            value = fir(tall, sets, *work, at + TILE - half, rows, counts).astype(BF16)
            out[pl.ds(at - done, rows), :] = value
            for t in range(tiles):
                turn(jnp.minimum((i + 1) * tiles + 1 + t, size // TILE - 1))
            return carry

        lax.fori_loop(done // rows, (done + out.shape[0]) // rows, block, 0)
        done += out.shape[0]


def whiten_part(taps, traces, sets, beside, after, pieces, inner):
    chans = traces.shape[0]
    size = sum(pieces)
    rows = 2 * TILE
    return pl.pallas_call(
        functools.partial(whiten_part_kernel, taps, rows, inner),
        out_shape=tuple(jax.ShapeDtypeStruct((piece, chans), BF16) for piece in pieces),
        in_specs=vmem(3) + [ANY],
        out_specs=tuple(vmem(len(pieces))),
        scratch_shapes=[pltpu.VMEM((size + 2 * TILE, chans), F32)] + fir_scratch(rows, chans),
        compiler_params=params(),
        cost_estimate=light(),
        name="whiten_inner" if inner else "whiten_outer",
    )(traces, sets, beside, after)


def order_kernel(ring, count, choose, after, *refs):
    parts, (*outs, gathered) = refs[:count], refs[count:]
    step = parts[0].shape[0]
    for i, part in enumerate(parts):
        gathered[i * step : (i + 1) * step, :] = part[...]
    if not ring:
        outs[0][...] = jnp.dot(choose[...].astype(BF16), gathered[...], preferred_element_type=F32).astype(BF16)
        return
    own, *sends = outs
    half, length = own.shape[0], sends[0].shape[1]
    here = lax.axis_index("tm")
    mine = choose[pl.ds(pl.multiple_of(here * half, half), half), :]
    few = half // 2
    other = (1 - here) * half + lax.axis_index("sub") * few
    theirs = choose[pl.ds(pl.multiple_of(other, few), few), :]
    wanted = jnp.concatenate([mine, theirs], 0).astype(BF16)
    got = jnp.dot(wanted, gathered[...], preferred_element_type=F32).astype(BF16)
    own[:, 0:TILE] = jnp.zeros((half, TILE), BF16)
    own[:, TILE + length :] = jnp.zeros((half, TILE), BF16)
    own[:, TILE : TILE + length] = got[:half]
    size = sends[0].shape[0]
    for n, send in enumerate(sends):
        send[...] = got[half + n * size : half + (n + 1) * size]


def order(choose, after, parts, ring):
    partners, total = choose.shape
    length = parts[0].shape[1]
    if ring:
        half = partners // 2
        out_shape = (
            jax.ShapeDtypeStruct((half, length + 2 * TILE), BF16),
            *[jax.ShapeDtypeStruct((half // ARRIVED, length), BF16)] * (ARRIVED // 2),
        )
        out_specs = tuple(vmem(1 + ARRIVED // 2))
    else:
        out_shape = jax.ShapeDtypeStruct((partners, length), BF16)
        out_specs = vmem(1)[0]
    return pl.pallas_call(
        functools.partial(order_kernel, ring, len(parts)),
        out_shape=out_shape,
        in_specs=vmem(1) + [ANY] + vmem(len(parts)),
        out_specs=out_specs,
        scratch_shapes=[pltpu.VMEM((total, length), BF16)],
        compiler_params=params(),
        cost_estimate=light(),
        name="order_partners",
    )(choose, after, *parts)


def lay_out(part, out, start, width):
    rows = part.shape[0]
    lane = lax.broadcasted_iota(jnp.int32, (rows, TILE), 1)
    tiles = [part[:, pl.ds(start + TILE * i, TILE)] for i in range(width // TILE + 1)]
    half = (LAGS - 1) // 2
    for b in range(FINE + 1):
        turned = [pltpu.roll(tile, half - b, 1) for tile in tiles]
        for i in range(width // TILE):
            piece = jnp.where(lane < half - b, turned[i], turned[i + 1])
            out[b * rows : (b + 1) * rows, TILE * i : TILE * i + TILE] = piece


def add_lags(shifted, chan, total, start, width, rows):
    chans = chan.shape[1]
    coarse = (LAGS - 1) // FINE
    pair = 2 if chans % TILE == 0 else 1
    for a in range(0, coarse, pair):
        cols = [chan[pl.ds(start + TILE - FINE * (a + i), width), :] for i in range(pair)]
        last = a + pair == coarse
        used = rows * (FINE + 1 if last else FINE)
        block = cols[0] if pair == 1 else jnp.concatenate(cols, 1)
        term = jnp.dot(shifted[:used, :], block, preferred_element_type=F32)
        for i in range(pair):
            size = used if i == pair - 1 else rows * FINE
            place = (a + i) * FINE * rows
            total[place : place + size, :] += term[:size, i * chans : (i + 1) * chans]


def correlate_all(part, chan, total, spare, start, width, chunk, rows):
    first, second, rest = spare
    whole = width // (2 * chunk) * (2 * chunk)
    lay_out(part, first, start, chunk)

    def advance(i, carry):
        now = pl.multiple_of(start + 2 * chunk * i, TILE)
        lay_out(part, second, now + chunk, chunk)
        add_lags(first, chan, total, now, chunk, rows)
        after = pl.multiple_of(jnp.minimum(now + 2 * chunk, start + whole - chunk), TILE)
        lay_out(part, first, after, chunk)
        add_lags(second, chan, total, now + chunk, chunk, rows)
        return carry

    lax.fori_loop(0, whole // (2 * chunk), advance, 0)
    if width > whole:
        lay_out(part, rest, start + whole, width - whole)
        add_lags(rest, chan, total, start + whole, width - whole, rows)


def add_pair(shifted, chan, before, total, start, width, rows, a, scale):
    chans = chan.shape[1]
    last = a + 2 == (LAGS - 1) // FINE
    used = rows * (FINE + 1 if last else FINE)
    term = None
    for copies, begin in zip(shifted, start):
        cols = [chan[pl.ds(begin + TILE - FINE * (a + i), width), :] for i in range(2)]
        piece = jnp.dot(copies[:used, :width], jnp.concatenate(cols, 1), preferred_element_type=F32)
        term = piece if term is None else term + piece
    for i in range(2):
        size = used if i == 1 else rows * FINE
        place = (a + i) * FINE * rows
        mine = term[:size, i * chans : (i + 1) * chans]
        if before is not None:
            mine = before[place : place + size, :] + mine
        total[place : place + size, :] = mine if scale is None else mine * scale


def correlate_ring(part, chan, total, spare, start, width, chunk, rows, ready, before, scale, out, sems):
    pairs = range(0, (LAGS - 1) // FINE, 2)
    rest = width % chunk
    count = width // chunk
    begin = [pl.multiple_of(start + rest + i * chunk, TILE) for i in range(count)]
    buffers = [spare[3] if rest and i == 0 else spare[i % 3] for i in range(count)]
    widths = [chunk + rest if i == 0 else chunk for i in range(count)]
    begin[0] = start
    lay_out(part, buffers[0], start, widths[0])
    for copy in ready:
        copy.wait()
    for i in range(count - 2):
        lay_out(part, buffers[i + 1], begin[i + 1], chunk)
        if i == count - 3:
            lay_out(part, buffers[i + 2], begin[i + 2], chunk)
        for a in pairs:
            add_pair([buffers[i]], chan, before, total, [begin[i]], widths[i], rows, a, None)
        before = total
    stores = []
    for n, a in enumerate(pairs):
        ends = (count - 2, count - 1)
        add_pair([buffers[i] for i in ends], chan, before, total, [begin[i] for i in ends], chunk, rows, a, scale)
        if out is not None:
            at = 2 * n * FINE * rows
            size = rows * (2 * FINE + (1 if a + 2 == (LAGS - 1) // FINE else 0))
            stores.append(pltpu.make_async_copy(total.at[pl.ds(at, size), :], out.at[pl.ds(at, size), :], sems.at[n]))
            stores[-1].start()
    for store in stores:
        store.wait()


def place_pieces(at_start, pieces, chan, length, sems):
    outer = pieces[0].shape[0]
    at = jnp.where(at_start, 0, length - outer)
    copies = []
    for n, piece in enumerate(pieces):
        size = piece.shape[0]
        to = chan.at[pl.ds(pl.multiple_of(TILE + at, TILE), size), :]
        copies.append(pltpu.make_async_copy(piece, to, sems.at[4 + n]))
        copies[-1].start()
        at = jnp.where(at_start, outer, 0) if n == 0 else at + size
    return copies


def first_kernel(chunk, count, part, *refs):
    pieces, (total, chan, a, b, c, d, sems) = refs[:count], refs[count:]
    length = part.shape[1] - 2 * TILE
    here = lax.axis_index("tm")
    ready = place_pieces(here == 0, pieces, chan, length, sems)
    edge = jnp.zeros((TILE, chan.shape[1]), BF16)
    chan[0:TILE, :] = edge
    chan[TILE + length :, :] = edge
    start = pl.multiple_of(here * TILE, TILE)
    correlate_ring(part, chan, total, (a, b, c, d), start, length, chunk, part.shape[0], ready, None, None, None, sems)


def second_kernel(chunk, scale, count, own_part, *refs):
    arrived, (own_head, own_tail, before, *refs) = refs[:ARRIVED], refs[ARRIVED:]
    pieces, (out, total, part, chan, a, b, c, d, sems) = refs[:count], refs[count:]
    length = part.shape[1] - 2 * TILE
    rows = part.shape[0]
    here = lax.axis_index("tm")
    ready = place_pieces(here > 0, pieces, chan, length, sems)
    later = here > 0
    few = arrived[0].shape[0]
    core = lax.axis_index("sub")
    for n, piece in enumerate(arrived):
        n = n + core * ARRIVED // 2
        at = jnp.where(n < ARRIVED, n, n - ARRIVED) * few
        part[pl.ds(pl.multiple_of(at, few), few), TILE : TILE + length] = piece[...]
    part[:, 0:TILE] = jnp.where(later, 0, own_part[:, length : length + TILE]).astype(BF16)
    part[:, TILE + length :] = jnp.where(later, own_part[:, TILE : 2 * TILE], 0).astype(BF16)
    chan[0:TILE, :] = jnp.where(later, 0, own_tail[own_tail.shape[0] - TILE :, :]).astype(BF16)
    chan[TILE + length :, :] = jnp.where(later, own_head[0:TILE, :], 0).astype(BF16)
    correlate_ring(part, chan, total, (a, b, c, d), 0, length + TILE, chunk, rows, ready, before, scale, out, sems)


def whole_kernel(chunk, scale, part_in, chan_in, total, part, chan, a, b, c):
    length = chan_in.shape[0]
    rows = part.shape[0]
    part[:, 0:TILE] = jnp.zeros((rows, TILE), BF16)
    part[:, TILE + length :] = jnp.zeros((rows, TILE), BF16)
    part[:, TILE : TILE + length] = part_in[...]
    edge = jnp.zeros((TILE, chan.shape[1]), BF16)
    chan[0:TILE, :] = edge
    chan[TILE + length :, :] = edge
    chan[TILE : TILE + length, :] = chan_in[...]
    total[...] = jnp.zeros_like(total)
    correlate_all(part, chan, total, (a, b, c), 0, length + TILE, chunk, rows)
    total[...] = total[...] * scale


def spare(rows, widths):
    return [pltpu.VMEM((rows * (FINE + 1), width), BF16) for width in widths]


def shifted(array, axis, step):
    count = lax.axis_size(axis)
    return lax.ppermute(array, axis, [(i, (i + step) % count) for i in range(count)])


def on_device(traces, filters, sources):
    chans, length = traces.shape
    partners = sources.shape[0]
    sizes = tuple(lax.axis_size(axis) for axis in ("tm", "chan", "sub"))
    time_devs, chan_devs, sub_devs = sizes
    slots = min(chans, MOST)
    rows = partners // time_devs
    scale = 1.0 / math.sqrt(length * time_devs)
    chunk = 4 * TILE
    taps = filters.T
    ring = time_devs == 2 and sub_devs == 2 and chan_devs <= 4 and chans % TILE == 0
    out_shape = jax.ShapeDtypeStruct((LAGS * rows, chans), F32)
    count = taps.shape[0]
    slot_rows, sets, chan_taps, choose, held = prepare(sizes, sources, taps, traces, slots, ring)
    if ring:
        here = lax.axis_index("tm")
        edge = lax.dynamic_slice_in_dim(traces, jnp.where(here == 0, length - TILE, 0), TILE, 1)
        beside = shifted(edge, "tm", 1)
        far = length // 2
        outer = whiten_part(count, held, sets, beside, beside, (far,), False)
        other_outer = [shifted(piece, "tm", 1) for piece in outer]
        picked = whiten_slots(sizes, count, slot_rows, held, beside, beside, chan_taps, outer[0], slots)
        inner = whiten_part(count, held, sets, beside, picked, (length - far,), True)
        other_inner = [shifted(piece, "tm", 1) for piece in inner]
        mine = [picked] + [shifted(picked, "chan", step) for step in range(1, chan_devs)]
        theirs = [shifted(part, "sub", 1) for part in mine]
        own_part, *send = order(choose, other_outer[0], [*mine, *theirs], True)
        near_rows = [shifted(part, "tm", 1) for part in send]
        pieces = len(outer) + len(inner)
        before = pl.pallas_call(
            functools.partial(first_kernel, chunk, pieces),
            out_shape=out_shape,
            in_specs=vmem(1) + [ANY] * pieces,
            out_specs=vmem(1)[0],
            scratch_shapes=[pltpu.VMEM((length + 2 * TILE, chans), BF16)]
            + spare(rows, (chunk, chunk, chunk, chunk + TILE))
            + [pltpu.SemaphoreType.DMA((4 + pieces,))],
            compiler_params=params(),
            cost_estimate=light(),
            name="correlate_own",
        )(own_part, *outer, *inner)
        near_rows, other_inner, before = lax.optimization_barrier((near_rows, other_inner, before))
        far_rows = [shifted(part, "sub", 1) for part in near_rows]
        total = pl.pallas_call(
            functools.partial(second_kernel, chunk, scale, pieces),
            out_shape=out_shape,
            in_specs=vmem(4 + 2 * len(send)) + [ANY] * pieces,
            out_specs=ANY,
            scratch_shapes=[
                pltpu.VMEM(out_shape.shape, F32),
                pltpu.VMEM((rows, length + 2 * TILE), BF16),
                pltpu.VMEM((length + 2 * TILE, chans), BF16),
            ]
            + spare(rows, (chunk, chunk, chunk, chunk + TILE))
            + [pltpu.SemaphoreType.DMA((4 + pieces,))],
            compiler_params=params(),
            cost_estimate=light(),
            name="correlate_other",
        )(own_part, *near_rows, *far_rows, inner[0], inner[-1], before, *other_outer, *other_inner)
    else:
        low = lax.ppermute(traces[:, length - TILE :], "tm", [(i, i + 1) for i in range(time_devs - 1)])
        high = lax.ppermute(traces[:, :TILE], "tm", [(i + 1, i) for i in range(time_devs - 1)])
        picked = whiten_slots(sizes, count, slot_rows, held, low, high, chan_taps, low, slots)
        whitened = whiten(time_devs, count, traces, low, high, sets)
        gathered = lax.all_gather(picked, ("chan", "sub"), axis=0, tiled=True)
        all_parts = order(choose, low, [gathered], False)
        parts = lax.all_to_all(all_parts, "tm", 0, 1, tiled=True)
        all_chans = lax.all_gather(whitened, "tm", axis=0, tiled=True)
        full = length * time_devs
        total = pl.pallas_call(
            functools.partial(whole_kernel, chunk, scale),
            out_shape=out_shape,
            in_specs=vmem(2),
            out_specs=vmem(1)[0],
            scratch_shapes=[
                pltpu.VMEM((rows, full + 2 * TILE), BF16),
                pltpu.VMEM((full + 2 * TILE, chans), BF16),
            ]
            + spare(rows, (chunk, chunk, TILE)),
            compiler_params=pltpu.CompilerParams(vmem_limit_bytes=2 * VMEM_BYTES),
            name="correlate_whole",
        )(parts, all_chans)
    return jnp.transpose(total.reshape(LAGS, rows, chans), (1, 0, 2))


def solution(mesh):
    return jax.shard_map(
        on_device,
        mesh=mesh,
        in_specs=(
            P(("groups", "chan", "sub"), "tm"),
            P(("groups", "chan", "sub"), None),
            P("groups"),
        ),
        out_specs=P("tm", None, ("groups", "chan", "sub")),
        check_vma=False,
    )
```

```python
import functools
import math

import jax
import jax.numpy as jnp
from jax import lax
from jax.experimental import pallas as pl
from jax.experimental.pallas import tpu as pltpu
from jax.sharding import PartitionSpec as P

LAGS = 129
MOST = 16
TILE = 128
FINE = 16
SETS = 24
ARRIVED = 2
F32 = jnp.float32
BF16 = jnp.bfloat16
VMEM_BYTES = 24 * 2**20


def vmem(count):
    return [pl.BlockSpec(memory_space=pltpu.VMEM)] * count


SMEM = pl.BlockSpec(memory_space=pltpu.SMEM)
ANY = pl.BlockSpec(memory_space=pl.ANY)


def params():
    return pltpu.CompilerParams(vmem_limit_bytes=VMEM_BYTES)


def light():
    return pl.CostEstimate(flops=1000, bytes_accessed=1000, transcendentals=0)


def set_sizes(taps):
    sizes = []
    for group in ((taps + 1) // 2, taps // 2, (taps + 1) // 2):
        sizes += [(group + 1) // 2, group // 2, (group + 1) // 2]
    return sizes


def split_taps(filters, sets, taps):
    def take(rows):
        return [filters[k : k + 1, :] if k < taps else None for k in rows]

    def plus(a, b):
        return [x if y is None else (y if x is None else x + y) for x, y in zip(a, b)]

    whole = 2 * ((taps + 1) // 2)
    even, odd = take(range(0, whole, 2)), take(range(1, whole, 2))
    for i, group in enumerate((even, odd, plus(even, odd))):
        group = group + [None] * (len(group) % 2)
        first, second = group[0::2], group[1::2]
        for j, rows in enumerate((first, second, plus(first, second))):
            for k, row in enumerate(rows):
                if row is not None:
                    at = SETS * (3 * i + j) + k
                    sets[at : at + 1, :] = row


def part_fir(stage, at, sets, row, count, rows):
    total = None
    for first in range(8):
        later = [j for j in range((count + 7) // 8) if first + 8 * j < count]
        window = stage[at + first : at + first + rows + 8 * later[-1], :]
        for j in later:
            k = row + first + 8 * j
            term = sets[k : k + 1, :] * window[8 * j : 8 * j + rows]
            total = term if total is None else total + term
    return total


def fir(samples, sets, stage, late, mixed, base, rows, counts):
    few = rows // 4
    extent = few + 32
    x3, x4, x5, x6 = (samples[pl.ds(base - 32 + p, extent, stride=4), :] for p in (3, 4, 5, 6))
    arrays = (x6, x4, x6 + x4, x5, x3, x5 + x3, x6 + x5, x4 + x3, (x6 + x4) + (x5 + x3))
    for i, array in enumerate(arrays):
        stage[i * extent : (i + 1) * extent, :] = array

    def halves(i, lead):
        size = few + lead
        at = 3 * i * extent
        p0 = part_fir(stage, at, sets, SETS * 3 * i, counts[3 * i], few + 8)
        p1 = part_fir(stage, at + extent + 8 - lead, sets, SETS * (3 * i + 1), counts[3 * i + 1], size)
        p2 = part_fir(stage, at + 2 * extent + 8 - lead, sets, SETS * (3 * i + 2), counts[3 * i + 2], size)
        late[8 : 16 + few, :] = p0
        return late[15 - lead : 15 - lead + size, :] + p1, p2 - p1 - late[16 - lead : 16 - lead + size, :]

    a_even, a_odd = halves(0, 8)
    b_even, b_odd = halves(1, 0)
    c_even, c_odd = halves(2, 0)
    mixed[0 : few + 8, :] = a_odd
    y0 = mixed[7 : 7 + few, :] + b_even
    y1 = c_even - a_even[8:] - b_even
    y2 = a_even[8:] + b_odd
    y3 = c_odd - a_odd[8:] - b_odd
    for p, y in enumerate((y0, y1, y2, y3)):
        mixed[pl.ds(p, few, stride=4), :] = y
    return mixed[0:rows, :]


def fir_scratch(rows, lanes):
    few = rows // 4
    return [
        pltpu.VMEM((9 * (few + 32), lanes), F32),
        pltpu.VMEM((few + 16, lanes), F32),
        pltpu.VMEM((max(rows, few + 8), lanes), F32),
    ]


def place_of(axes, sizes):
    at = 0
    for axis, size in zip(axes, sizes):
        at = at * size + lax.axis_index(axis)
    return at


def prepare_kernel(sizes, chans, ring, slots, sources, sources_row, filters, _, rows, sets, chan_taps, wanted, same):
    taps = filters.shape[0]
    first_chan = place_of(("chan", "sub"), sizes[1:]) * chans
    for s in range(slots):
        rows[s] = 0

    def find(p, count):
        local = sources[p] - first_chan
        mine = (local >= 0) & (local < chans)
        rows[jnp.where(mine, count, slots)] = local
        return count + mine.astype(jnp.int32)

    lax.fori_loop(0, sources.shape[0], find, 0, unroll=16)
    split_taps(filters, sets, taps)
    chan_taps[...] = jnp.concatenate([filters[...], jnp.zeros((TILE - taps, chans), F32)], 0).T
    partners = sources_row.shape[1]
    _, chan_devs, sub_devs = sizes
    own_row = jnp.broadcast_to(sources_row[...].astype(F32), (partners, partners))
    owner_row = jnp.floor((own_row + 0.5) * (1.0 / chans))
    owner_col = owner_row.T
    lane = lax.broadcasted_iota(jnp.int32, (partners, partners), 1)
    line = lax.broadcasted_iota(jnp.int32, (partners, partners), 0)
    earlier = (owner_row == owner_col) & (lane < line)
    rank = jnp.sum(earlier.astype(F32), axis=1, keepdims=True)
    owner = owner_col[:, 0:1]
    if ring:
        owner_chan = jnp.floor((owner + 0.5) * (1.0 / sub_devs))
        owner_sub = owner - sub_devs * owner_chan
        my_chan = lax.axis_index("chan").astype(F32)
        my_sub = lax.axis_index("sub").astype(F32)
        behind = my_chan - owner_chan
        behind = jnp.where(behind < 0, behind + chan_devs, behind)
        place = jnp.where(owner_sub == my_sub, 0.0, 1.0) * chan_devs + behind
    else:
        place = owner
    at = lax.broadcasted_iota(jnp.int32, wanted.shape, 1).astype(F32)
    wanted[...] = (place * slots + rank == at).astype(F32)


def prepare(sizes, sources, filters, traces, slots, ring):
    taps, chans = filters.shape
    partners = sources.shape[0]
    total = slots * sizes[1] * sizes[2]
    return pl.pallas_call(
        functools.partial(prepare_kernel, sizes, chans, ring, slots),
        out_shape=(
            jax.ShapeDtypeStruct((slots + 1,), jnp.int32),
            jax.ShapeDtypeStruct((9 * SETS, chans), F32),
            jax.ShapeDtypeStruct((chans, TILE), F32),
            jax.ShapeDtypeStruct((partners, total), F32),
            jax.ShapeDtypeStruct(traces.shape, F32),
        ),
        in_specs=[SMEM] + vmem(2) + [ANY],
        out_specs=(SMEM, *vmem(3), ANY),
        input_output_aliases={3: 4},
        compiler_params=params(),
        cost_estimate=light(),
        name="prepare",
    )(sources, sources.reshape(1, partners), filters, traces)


def slots_kernel(taps, sizes, rows, x, low, high, chan_taps, after, out, wide, tall, lane_taps, *work):
    chans, length = x.shape
    slots = out.shape[0]
    segs = TILE // slots
    seg_len = length // segs
    half = (taps - 1) // 2
    here = lax.axis_index("tm")
    keep_low = (here > 0).astype(F32)
    keep_high = (here < sizes[0] - 1).astype(F32)
    for s in range(slots):
        row = rows[s]
        group = pl.multiple_of((row >> 3) << 3, 8)
        turn = (s - row) & 7

        def pick(ref):
            return pltpu.roll(ref[pl.ds(group, 8), :], turn, 0)[s % 8 : s % 8 + 1, :]

        wide[s : s + 1, 0:TILE] = pick(low) * keep_low
        wide[s : s + 1, TILE : TILE + length] = pick(x)
        wide[s : s + 1, TILE + length :] = pick(high) * keep_high
        lane_taps[s : s + 1, :] = pick(chan_taps)
    picked = lane_taps[0:slots, :]
    lane_taps[...] = jnp.concatenate([picked] * segs, 0).T
    for t in range(seg_len // TILE + 2):
        cols = [wide[:, g * seg_len + t * TILE : g * seg_len + (t + 1) * TILE] for g in range(segs)]
        tall[t * TILE : (t + 1) * TILE, :] = jnp.concatenate(cols, 0).T
    split_taps(lane_taps, work[0], taps)
    counts = set_sizes(taps)
    done = fir(tall, *work, TILE - half, seg_len, counts)
    for t in range(seg_len // TILE):
        turned = done[t * TILE : (t + 1) * TILE].T
        for g in range(segs):
            start = g * seg_len + t * TILE
            out[:, start : start + TILE] = turned[g * slots : (g + 1) * slots].astype(BF16)


def whiten_slots(sizes, taps, rows, traces, low, high, chan_taps, after, slots):
    length = traces.shape[1]
    seg_len = length * slots // TILE
    return pl.pallas_call(
        functools.partial(slots_kernel, taps, sizes),
        out_shape=jax.ShapeDtypeStruct((slots, length), BF16),
        in_specs=[SMEM] + vmem(4) + [ANY],
        out_specs=vmem(1)[0],
        scratch_shapes=[
            pltpu.VMEM((slots, length + 2 * TILE), F32),
            pltpu.VMEM((seg_len + 2 * TILE, TILE), F32),
            pltpu.VMEM((TILE, TILE), F32),
        ]
        + [pltpu.VMEM((9 * SETS, TILE), F32)]
        + fir_scratch(seg_len, TILE),
        compiler_params=params(),
        cost_estimate=light(),
        name="whiten_slots",
    )(rows, traces, low, high, chan_taps, after)


def whiten_kernel(taps, rows, time_devs, x, low, high, sets, out, tall, *work):
    length = x.shape[1]
    half = (taps - 1) // 2
    here = lax.axis_index("tm")
    tall[0:TILE, :] = jnp.where(here > 0, low[...], 0.0).T
    tall[TILE + length :, :] = jnp.where(here < time_devs - 1, high[...], 0.0).T
    counts = set_sizes(taps)

    def turn(t, carry):
        start = pl.multiple_of(t * TILE, TILE)
        tall[pl.ds(start + TILE, TILE), :] = x[:, pl.ds(start, TILE)].T
        return carry

    lax.fori_loop(0, length // TILE, turn, 0)

    def block(i, carry):
        at = pl.multiple_of(i * rows, rows)
        out[pl.ds(at, rows), :] = fir(tall, sets, *work, at + TILE - half, rows, counts).astype(BF16)
        return carry

    lax.fori_loop(0, length // rows, block, 0)


def whiten(time_devs, taps, traces, low, high, sets):
    chans, length = traces.shape
    rows = 2 * TILE
    return pl.pallas_call(
        functools.partial(whiten_kernel, taps, rows, time_devs),
        out_shape=jax.ShapeDtypeStruct((length, chans), BF16),
        in_specs=vmem(4),
        out_specs=vmem(1)[0],
        scratch_shapes=[pltpu.VMEM((length + 2 * TILE, chans), F32)] + fir_scratch(rows, chans),
        compiler_params=params(),
        cost_estimate=light(),
        name="whiten",
    )(traces, low, high, sets)


def whiten_part_kernel(taps, rows, inner, x, sets, beside, _, *refs):
    outs, (tall, *work) = refs[:-4], refs[-4:]
    length, size = x.shape[1], tall.shape[0] - 2 * TILE
    half = (taps - 1) // 2
    tiles = rows // TILE
    at_start = (lax.axis_index("tm") > 0) == inner
    start = jnp.where(at_start, 0, length - size)
    near = x[:, pl.ds(pl.multiple_of(jnp.where(at_start, size, length - size - TILE), TILE), TILE)]
    outside = beside[...] if inner else jnp.zeros_like(near)
    tall[0:TILE, :] = jnp.where(at_start, outside, near).T
    tall[TILE + size :, :] = jnp.where(at_start, near, outside).T
    counts = set_sizes(taps)

    def turn(t):
        tall[pl.ds(pl.multiple_of(t * TILE + TILE, TILE), TILE), :] = x[
            :, pl.ds(pl.multiple_of(start + t * TILE, TILE), TILE)
        ].T

    for t in range(tiles + 1):
        turn(t)

    done = 0
    for out in outs:

        def block(i, carry):
            at = pl.multiple_of(i * rows, rows)
            value = fir(tall, sets, *work, at + TILE - half, rows, counts).astype(BF16)
            out[pl.ds(at - done, rows), :] = value
            for t in range(tiles):
                turn(jnp.minimum((i + 1) * tiles + 1 + t, size // TILE - 1))
            return carry

        lax.fori_loop(done // rows, (done + out.shape[0]) // rows, block, 0)
        done += out.shape[0]


def whiten_part(taps, traces, sets, beside, after, pieces, inner):
    chans = traces.shape[0]
    size = sum(pieces)
    rows = 2 * TILE
    return pl.pallas_call(
        functools.partial(whiten_part_kernel, taps, rows, inner),
        out_shape=tuple(jax.ShapeDtypeStruct((piece, chans), BF16) for piece in pieces),
        in_specs=vmem(3) + [ANY],
        out_specs=tuple(vmem(len(pieces))),
        scratch_shapes=[pltpu.VMEM((size + 2 * TILE, chans), F32)] + fir_scratch(rows, chans),
        compiler_params=params(),
        cost_estimate=light(),
        name="whiten_inner" if inner else "whiten_outer",
    )(traces, sets, beside, after)


def order_kernel(ring, count, choose, after, *refs):
    parts, (*outs, gathered) = refs[:count], refs[count:]
    step = parts[0].shape[0]
    for i, part in enumerate(parts):
        gathered[i * step : (i + 1) * step, :] = part[...]
    if not ring:
        outs[0][...] = jnp.dot(choose[...].astype(BF16), gathered[...], preferred_element_type=F32).astype(BF16)
        return
    own, *sends = outs
    half, length = own.shape[0], sends[0].shape[1]
    here = lax.axis_index("tm")
    mine = choose[pl.ds(pl.multiple_of(here * half, half), half), :]
    few = half // 2
    other = (1 - here) * half + lax.axis_index("sub") * few
    theirs = choose[pl.ds(pl.multiple_of(other, few), few), :]
    wanted = jnp.concatenate([mine, theirs], 0).astype(BF16)
    got = jnp.dot(wanted, gathered[...], preferred_element_type=F32).astype(BF16)
    own[:, 0:TILE] = jnp.zeros((half, TILE), BF16)
    own[:, TILE + length :] = jnp.zeros((half, TILE), BF16)
    own[:, TILE : TILE + length] = got[:half]
    size = sends[0].shape[0]
    for n, send in enumerate(sends):
        send[...] = got[half + n * size : half + (n + 1) * size]


def order(choose, after, parts, ring):
    partners, total = choose.shape
    length = parts[0].shape[1]
    if ring:
        half = partners // 2
        out_shape = (
            jax.ShapeDtypeStruct((half, length + 2 * TILE), BF16),
            *[jax.ShapeDtypeStruct((half // ARRIVED, length), BF16)] * (ARRIVED // 2),
        )
        out_specs = tuple(vmem(1 + ARRIVED // 2))
    else:
        out_shape = jax.ShapeDtypeStruct((partners, length), BF16)
        out_specs = vmem(1)[0]
    return pl.pallas_call(
        functools.partial(order_kernel, ring, len(parts)),
        out_shape=out_shape,
        in_specs=vmem(1) + [ANY] + vmem(len(parts)),
        out_specs=out_specs,
        scratch_shapes=[pltpu.VMEM((total, length), BF16)],
        compiler_params=params(),
        cost_estimate=light(),
        name="order_partners",
    )(choose, after, *parts)


def lay_out(part, out, start, width):
    rows = part.shape[0]
    lane = lax.broadcasted_iota(jnp.int32, (rows, TILE), 1)
    tiles = [part[:, pl.ds(start + TILE * i, TILE)] for i in range(width // TILE + 1)]
    half = (LAGS - 1) // 2
    for b in range(FINE + 1):
        turned = [pltpu.roll(tile, half - b, 1) for tile in tiles]
        for i in range(width // TILE):
            piece = jnp.where(lane < half - b, turned[i], turned[i + 1])
            out[b * rows : (b + 1) * rows, TILE * i : TILE * i + TILE] = piece


def add_lags(shifted, chan, total, start, width, rows):
    chans = chan.shape[1]
    coarse = (LAGS - 1) // FINE
    pair = 2 if chans % TILE == 0 else 1
    for a in range(0, coarse, pair):
        cols = [chan[pl.ds(start + TILE - FINE * (a + i), width), :] for i in range(pair)]
        last = a + pair == coarse
        used = rows * (FINE + 1 if last else FINE)
        block = cols[0] if pair == 1 else jnp.concatenate(cols, 1)
        term = jnp.dot(shifted[:used, :], block, preferred_element_type=F32)
        for i in range(pair):
            size = used if i == pair - 1 else rows * FINE
            place = (a + i) * FINE * rows
            total[place : place + size, :] += term[:size, i * chans : (i + 1) * chans]


def correlate_all(part, chan, total, spare, start, width, chunk, rows):
    first, second, rest = spare
    whole = width // (2 * chunk) * (2 * chunk)
    lay_out(part, first, start, chunk)

    def advance(i, carry):
        now = pl.multiple_of(start + 2 * chunk * i, TILE)
        lay_out(part, second, now + chunk, chunk)
        add_lags(first, chan, total, now, chunk, rows)
        after = pl.multiple_of(jnp.minimum(now + 2 * chunk, start + whole - chunk), TILE)
        lay_out(part, first, after, chunk)
        add_lags(second, chan, total, now + chunk, chunk, rows)
        return carry

    lax.fori_loop(0, whole // (2 * chunk), advance, 0)
    if width > whole:
        lay_out(part, rest, start + whole, width - whole)
        add_lags(rest, chan, total, start + whole, width - whole, rows)


def add_pair(shifted, chan, before, total, start, width, rows, a, scale):
    chans = chan.shape[1]
    last = a + 2 == (LAGS - 1) // FINE
    used = rows * (FINE + 1 if last else FINE)
    term = None
    for copies, begin in zip(shifted, start):
        cols = [chan[pl.ds(begin + TILE - FINE * (a + i), width), :] for i in range(2)]
        piece = jnp.dot(copies[:used, :width], jnp.concatenate(cols, 1), preferred_element_type=F32)
        term = piece if term is None else term + piece
    for i in range(2):
        size = used if i == 1 else rows * FINE
        place = (a + i) * FINE * rows
        mine = term[:size, i * chans : (i + 1) * chans]
        if before is not None:
            mine = before[place : place + size, :] + mine
        total[place : place + size, :] = mine if scale is None else mine * scale


def correlate_ring(part, chan, total, spare, start, width, chunk, rows, ready, before, scale, out, sems):
    pairs = range(0, (LAGS - 1) // FINE, 2)
    rest = width % chunk
    count = width // chunk
    begin = [pl.multiple_of(start + rest + i * chunk, TILE) for i in range(count)]
    buffers = [spare[3] if rest and i == 0 else spare[i % 3] for i in range(count)]
    widths = [chunk + rest if i == 0 else chunk for i in range(count)]
    begin[0] = start
    lay_out(part, buffers[0], start, widths[0])
    for copy in ready:
        copy.wait()
    for i in range(count - 2):
        lay_out(part, buffers[i + 1], begin[i + 1], chunk)
        if i == count - 3:
            lay_out(part, buffers[i + 2], begin[i + 2], chunk)
        for a in pairs:
            add_pair([buffers[i]], chan, before, total, [begin[i]], widths[i], rows, a, None)
        before = total
    stores = []
    for n, a in enumerate(pairs):
        ends = (count - 2, count - 1)
        add_pair([buffers[i] for i in ends], chan, before, total, [begin[i] for i in ends], chunk, rows, a, scale)
        if out is not None:
            at = 2 * n * FINE * rows
            size = rows * (2 * FINE + (1 if a + 2 == (LAGS - 1) // FINE else 0))
            stores.append(pltpu.make_async_copy(total.at[pl.ds(at, size), :], out.at[pl.ds(at, size), :], sems.at[n]))
            stores[-1].start()
    for store in stores:
        store.wait()


def place_pieces(at_start, pieces, chan, length, sems):
    outer = pieces[0].shape[0]
    at = jnp.where(at_start, 0, length - outer)
    copies = []
    for n, piece in enumerate(pieces):
        size = piece.shape[0]
        to = chan.at[pl.ds(pl.multiple_of(TILE + at, TILE), size), :]
        copies.append(pltpu.make_async_copy(piece, to, sems.at[4 + n]))
        copies[-1].start()
        at = jnp.where(at_start, outer, 0) if n == 0 else at + size
    return copies


def first_kernel(chunk, count, part, *refs):
    pieces, (total, chan, a, b, c, d, sems) = refs[:count], refs[count:]
    length = part.shape[1] - 2 * TILE
    here = lax.axis_index("tm")
    ready = place_pieces(here == 0, pieces, chan, length, sems)
    edge = jnp.zeros((TILE, chan.shape[1]), BF16)
    chan[0:TILE, :] = edge
    chan[TILE + length :, :] = edge
    start = pl.multiple_of(here * TILE, TILE)
    correlate_ring(part, chan, total, (a, b, c, d), start, length, chunk, part.shape[0], ready, None, None, None, sems)


def second_kernel(chunk, scale, count, own_part, *refs):
    arrived, (own_head, own_tail, before, *refs) = refs[:ARRIVED], refs[ARRIVED:]
    pieces, (out, total, part, chan, a, b, c, d, sems) = refs[:count], refs[count:]
    length = part.shape[1] - 2 * TILE
    rows = part.shape[0]
    here = lax.axis_index("tm")
    ready = place_pieces(here > 0, pieces, chan, length, sems)
    later = here > 0
    few = arrived[0].shape[0]
    core = lax.axis_index("sub")
    for n, piece in enumerate(arrived):
        n = n + core * ARRIVED // 2
        at = jnp.where(n < ARRIVED, n, n - ARRIVED) * few
        part[pl.ds(pl.multiple_of(at, few), few), TILE : TILE + length] = piece[...]
    part[:, 0:TILE] = jnp.where(later, 0, own_part[:, length : length + TILE]).astype(BF16)
    part[:, TILE + length :] = jnp.where(later, own_part[:, TILE : 2 * TILE], 0).astype(BF16)
    chan[0:TILE, :] = jnp.where(later, 0, own_tail[own_tail.shape[0] - TILE :, :]).astype(BF16)
    chan[TILE + length :, :] = jnp.where(later, own_head[0:TILE, :], 0).astype(BF16)
    correlate_ring(part, chan, total, (a, b, c, d), 0, length + TILE, chunk, rows, ready, before, scale, out, sems)


def whole_kernel(chunk, scale, part_in, chan_in, total, part, chan, a, b, c):
    length = chan_in.shape[0]
    rows = part.shape[0]
    part[:, 0:TILE] = jnp.zeros((rows, TILE), BF16)
    part[:, TILE + length :] = jnp.zeros((rows, TILE), BF16)
    part[:, TILE : TILE + length] = part_in[...]
    edge = jnp.zeros((TILE, chan.shape[1]), BF16)
    chan[0:TILE, :] = edge
    chan[TILE + length :, :] = edge
    chan[TILE : TILE + length, :] = chan_in[...]
    total[...] = jnp.zeros_like(total)
    correlate_all(part, chan, total, (a, b, c), 0, length + TILE, chunk, rows)
    total[...] = total[...] * scale


def spare(rows, widths):
    return [pltpu.VMEM((rows * (FINE + 1), width), BF16) for width in widths]


def shifted(array, axis, step):
    count = lax.axis_size(axis)
    return lax.ppermute(array, axis, [(i, (i + step) % count) for i in range(count)])


def on_device(traces, filters, sources):
    chans, length = traces.shape
    partners = sources.shape[0]
    sizes = tuple(lax.axis_size(axis) for axis in ("tm", "chan", "sub"))
    time_devs, chan_devs, sub_devs = sizes
    slots = min(chans, MOST)
    rows = partners // time_devs
    scale = 1.0 / math.sqrt(length * time_devs)
    chunk = 4 * TILE
    taps = filters.T
    ring = time_devs == 2 and sub_devs == 2 and chan_devs <= 4 and chans % TILE == 0
    out_shape = jax.ShapeDtypeStruct((LAGS * rows, chans), F32)
    count = taps.shape[0]
    slot_rows, sets, chan_taps, choose, held = prepare(sizes, sources, taps, traces, slots, ring)
    if ring:
        here = lax.axis_index("tm")
        edge = lax.dynamic_slice_in_dim(traces, jnp.where(here == 0, length - TILE, 0), TILE, 1)
        beside = shifted(edge, "tm", 1)
        far = length // 2
        outer = whiten_part(count, held, sets, edge, edge, (far,), False)
        beside, *outer = lax.optimization_barrier((beside, *outer))
        other_outer = [shifted(piece, "tm", 1) for piece in outer]
        picked = whiten_slots(sizes, count, slot_rows, held, beside, beside, chan_taps, outer[0], slots)
        inner = whiten_part(count, held, sets, beside, picked, (length - far,), True)
        other_inner = [shifted(piece, "tm", 1) for piece in inner]
        mine = [picked] + [shifted(picked, "chan", step) for step in range(1, chan_devs)]
        theirs = [shifted(part, "sub", 1) for part in mine]
        own_part, *send = order(choose, other_outer[0], [*mine, *theirs], True)
        near_rows = [shifted(part, "tm", 1) for part in send]
        pieces = len(outer) + len(inner)
        before = pl.pallas_call(
            functools.partial(first_kernel, chunk, pieces),
            out_shape=out_shape,
            in_specs=vmem(1) + [ANY] * pieces,
            out_specs=vmem(1)[0],
            scratch_shapes=[pltpu.VMEM((length + 2 * TILE, chans), BF16)]
            + spare(rows, (chunk, chunk, chunk, chunk + TILE))
            + [pltpu.SemaphoreType.DMA((4 + pieces,))],
            compiler_params=params(),
            cost_estimate=light(),
            name="correlate_own",
        )(own_part, *outer, *inner)
        near_rows, other_inner, before = lax.optimization_barrier((near_rows, other_inner, before))
        far_rows = [shifted(part, "sub", 1) for part in near_rows]
        total = pl.pallas_call(
            functools.partial(second_kernel, chunk, scale, pieces),
            out_shape=out_shape,
            in_specs=vmem(4 + 2 * len(send)) + [ANY] * pieces,
            out_specs=ANY,
            scratch_shapes=[
                pltpu.VMEM(out_shape.shape, F32),
                pltpu.VMEM((rows, length + 2 * TILE), BF16),
                pltpu.VMEM((length + 2 * TILE, chans), BF16),
            ]
            + spare(rows, (chunk, chunk, chunk, chunk + TILE))
            + [pltpu.SemaphoreType.DMA((4 + pieces,))],
            compiler_params=params(),
            cost_estimate=light(),
            name="correlate_other",
        )(own_part, *near_rows, *far_rows, inner[0], inner[-1], before, *other_outer, *other_inner)
    else:
        low = lax.ppermute(traces[:, length - TILE :], "tm", [(i, i + 1) for i in range(time_devs - 1)])
        high = lax.ppermute(traces[:, :TILE], "tm", [(i + 1, i) for i in range(time_devs - 1)])
        picked = whiten_slots(sizes, count, slot_rows, held, low, high, chan_taps, low, slots)
        whitened = whiten(time_devs, count, traces, low, high, sets)
        gathered = lax.all_gather(picked, ("chan", "sub"), axis=0, tiled=True)
        all_parts = order(choose, low, [gathered], False)
        parts = lax.all_to_all(all_parts, "tm", 0, 1, tiled=True)
        all_chans = lax.all_gather(whitened, "tm", axis=0, tiled=True)
        full = length * time_devs
        total = pl.pallas_call(
            functools.partial(whole_kernel, chunk, scale),
            out_shape=out_shape,
            in_specs=vmem(2),
            out_specs=vmem(1)[0],
            scratch_shapes=[
                pltpu.VMEM((rows, full + 2 * TILE), BF16),
                pltpu.VMEM((full + 2 * TILE, chans), BF16),
            ]
            + spare(rows, (chunk, chunk, TILE)),
            compiler_params=pltpu.CompilerParams(vmem_limit_bytes=2 * VMEM_BYTES),
            name="correlate_whole",
        )(parts, all_chans)
    return jnp.transpose(total.reshape(LAGS, rows, chans), (1, 0, 2))


def solution(mesh):
    return jax.shard_map(
        on_device,
        mesh=mesh,
        in_specs=(
            P(("groups", "chan", "sub"), "tm"),
            P(("groups", "chan", "sub"), None),
            P("groups"),
        ),
        out_specs=P("tm", None, ("groups", "chan", "sub")),
        check_vma=False,
    )
```

```python
import functools
import math

import jax
import jax.numpy as jnp
from jax import lax
from jax.experimental import pallas as pl
from jax.experimental.pallas import tpu as pltpu
from jax.sharding import PartitionSpec as P

LAGS = 129
MOST = 16
TILE = 128
FINE = 16
SETS = 24
ARRIVED = 2
F32 = jnp.float32
BF16 = jnp.bfloat16
VMEM_BYTES = 24 * 2**20


def vmem(count):
    return [pl.BlockSpec(memory_space=pltpu.VMEM)] * count


SMEM = pl.BlockSpec(memory_space=pltpu.SMEM)
ANY = pl.BlockSpec(memory_space=pl.ANY)


def params():
    return pltpu.CompilerParams(vmem_limit_bytes=VMEM_BYTES)


def light():
    return pl.CostEstimate(flops=1000, bytes_accessed=1000, transcendentals=0)


def set_sizes(taps):
    sizes = []
    for group in ((taps + 1) // 2, taps // 2, (taps + 1) // 2):
        sizes += [(group + 1) // 2, group // 2, (group + 1) // 2]
    return sizes


def split_taps(filters, sets, taps):
    def take(rows):
        return [filters[k : k + 1, :] if k < taps else None for k in rows]

    def plus(a, b):
        return [x if y is None else (y if x is None else x + y) for x, y in zip(a, b)]

    whole = 2 * ((taps + 1) // 2)
    even, odd = take(range(0, whole, 2)), take(range(1, whole, 2))
    for i, group in enumerate((even, odd, plus(even, odd))):
        group = group + [None] * (len(group) % 2)
        first, second = group[0::2], group[1::2]
        for j, rows in enumerate((first, second, plus(first, second))):
            for k, row in enumerate(rows):
                if row is not None:
                    at = SETS * (3 * i + j) + k
                    sets[at : at + 1, :] = row


def part_fir(stage, at, sets, row, count, rows):
    total = None
    for first in range(8):
        later = [j for j in range((count + 7) // 8) if first + 8 * j < count]
        window = stage[at + first : at + first + rows + 8 * later[-1], :]
        for j in later:
            k = row + first + 8 * j
            term = sets[k : k + 1, :] * window[8 * j : 8 * j + rows]
            total = term if total is None else total + term
    return total


def fir(samples, sets, stage, late, mixed, base, rows, counts):
    few = rows // 4
    extent = few + 32
    x3, x4, x5, x6 = (samples[pl.ds(base - 32 + p, extent, stride=4), :] for p in (3, 4, 5, 6))
    arrays = (x6, x4, x6 + x4, x5, x3, x5 + x3, x6 + x5, x4 + x3, (x6 + x4) + (x5 + x3))
    for i, array in enumerate(arrays):
        stage[i * extent : (i + 1) * extent, :] = array

    def halves(i, lead):
        size = few + lead
        at = 3 * i * extent
        p0 = part_fir(stage, at, sets, SETS * 3 * i, counts[3 * i], few + 8)
        p1 = part_fir(stage, at + extent + 8 - lead, sets, SETS * (3 * i + 1), counts[3 * i + 1], size)
        p2 = part_fir(stage, at + 2 * extent + 8 - lead, sets, SETS * (3 * i + 2), counts[3 * i + 2], size)
        late[8 : 16 + few, :] = p0
        return late[15 - lead : 15 - lead + size, :] + p1, p2 - p1 - late[16 - lead : 16 - lead + size, :]

    a_even, a_odd = halves(0, 8)
    b_even, b_odd = halves(1, 0)
    c_even, c_odd = halves(2, 0)
    mixed[0 : few + 8, :] = a_odd
    y0 = mixed[7 : 7 + few, :] + b_even
    y1 = c_even - a_even[8:] - b_even
    y2 = a_even[8:] + b_odd
    y3 = c_odd - a_odd[8:] - b_odd
    for p, y in enumerate((y0, y1, y2, y3)):
        mixed[pl.ds(p, few, stride=4), :] = y
    return mixed[0:rows, :]


def fir_scratch(rows, lanes):
    few = rows // 4
    return [
        pltpu.VMEM((9 * (few + 32), lanes), F32),
        pltpu.VMEM((few + 16, lanes), F32),
        pltpu.VMEM((max(rows, few + 8), lanes), F32),
    ]


def place_of(axes, sizes):
    at = 0
    for axis, size in zip(axes, sizes):
        at = at * size + lax.axis_index(axis)
    return at


def choose_rows(sizes, chans, ring, slots, sources_row, wanted):
    partners = sources_row.shape[1]
    _, chan_devs, sub_devs = sizes
    own_row = jnp.broadcast_to(sources_row[...].astype(F32), (partners, partners))
    owner_row = jnp.floor((own_row + 0.5) * (1.0 / chans))
    owner_col = owner_row.T
    lane = lax.broadcasted_iota(jnp.int32, (partners, partners), 1)
    line = lax.broadcasted_iota(jnp.int32, (partners, partners), 0)
    earlier = (owner_row == owner_col) & (lane < line)
    rank = jnp.sum(earlier.astype(F32), axis=1, keepdims=True)
    owner = owner_col[:, 0:1]
    if ring:
        owner_chan = jnp.floor((owner + 0.5) * (1.0 / sub_devs))
        owner_sub = owner - sub_devs * owner_chan
        my_chan = lax.axis_index("chan").astype(F32)
        my_sub = lax.axis_index("sub").astype(F32)
        behind = my_chan - owner_chan
        behind = jnp.where(behind < 0, behind + chan_devs, behind)
        place = jnp.where(owner_sub == my_sub, 0.0, 1.0) * chan_devs + behind
    else:
        place = owner
    at = lax.broadcasted_iota(jnp.int32, wanted.shape, 1).astype(F32)
    wanted[...] = (place * slots + rank == at).astype(F32)


def prepare_kernel(sizes, chans, ring, slots, sources, sources_row, filters, _, rows, sets, chan_taps, same, *wanted):
    taps = filters.shape[0]
    first_chan = place_of(("chan", "sub"), sizes[1:]) * chans
    for s in range(slots):
        rows[s] = 0

    def find(p, count):
        local = sources[p] - first_chan
        mine = (local >= 0) & (local < chans)
        rows[jnp.where(mine, count, slots)] = local
        return count + mine.astype(jnp.int32)

    lax.fori_loop(0, sources.shape[0], find, 0, unroll=16)
    split_taps(filters, sets, taps)
    chan_taps[...] = jnp.concatenate([filters[...], jnp.zeros((TILE - taps, chans), F32)], 0).T
    if not ring:
        choose_rows(sizes, chans, ring, slots, sources_row, wanted[0])


def prepare(sizes, sources, filters, traces, slots, ring):
    taps, chans = filters.shape
    partners = sources.shape[0]
    total = slots * sizes[1] * sizes[2]
    return pl.pallas_call(
        functools.partial(prepare_kernel, sizes, chans, ring, slots),
        out_shape=(
            jax.ShapeDtypeStruct((slots + 1,), jnp.int32),
            jax.ShapeDtypeStruct((9 * SETS, chans), F32),
            jax.ShapeDtypeStruct((chans, TILE), F32),
            jax.ShapeDtypeStruct(traces.shape, F32),
            *[jax.ShapeDtypeStruct((partners, total), F32)] * (not ring),
        ),
        in_specs=[SMEM] + vmem(2) + [ANY],
        out_specs=(SMEM, *vmem(2), ANY, *vmem(not ring)),
        input_output_aliases={3: 3},
        compiler_params=params(),
        cost_estimate=light(),
        name="prepare",
    )(sources, sources.reshape(1, partners), filters, traces)


def slots_kernel(taps, sizes, rows, x, low, high, chan_taps, after, out, wide, tall, lane_taps, *work):
    chans, length = x.shape
    slots = out.shape[0]
    segs = TILE // slots
    seg_len = length // segs
    half = (taps - 1) // 2
    here = lax.axis_index("tm")
    keep_low = (here > 0).astype(F32)
    keep_high = (here < sizes[0] - 1).astype(F32)
    for s in range(slots):
        row = rows[s]
        group = pl.multiple_of((row >> 3) << 3, 8)
        turn = (s - row) & 7

        def pick(ref):
            return pltpu.roll(ref[pl.ds(group, 8), :], turn, 0)[s % 8 : s % 8 + 1, :]

        wide[s : s + 1, 0:TILE] = pick(low) * keep_low
        wide[s : s + 1, TILE : TILE + length] = pick(x)
        wide[s : s + 1, TILE + length :] = pick(high) * keep_high
        lane_taps[s : s + 1, :] = pick(chan_taps)
    picked = lane_taps[0:slots, :]
    lane_taps[...] = jnp.concatenate([picked] * segs, 0).T
    for t in range(seg_len // TILE + 2):
        cols = [wide[:, g * seg_len + t * TILE : g * seg_len + (t + 1) * TILE] for g in range(segs)]
        tall[t * TILE : (t + 1) * TILE, :] = jnp.concatenate(cols, 0).T
    split_taps(lane_taps, work[0], taps)
    counts = set_sizes(taps)
    done = fir(tall, *work, TILE - half, seg_len, counts)
    for t in range(seg_len // TILE):
        turned = done[t * TILE : (t + 1) * TILE].T
        for g in range(segs):
            start = g * seg_len + t * TILE
            out[:, start : start + TILE] = turned[g * slots : (g + 1) * slots].astype(BF16)


def whiten_slots(sizes, taps, rows, traces, low, high, chan_taps, after, slots):
    length = traces.shape[1]
    seg_len = length * slots // TILE
    return pl.pallas_call(
        functools.partial(slots_kernel, taps, sizes),
        out_shape=jax.ShapeDtypeStruct((slots, length), BF16),
        in_specs=[SMEM] + vmem(4) + [ANY],
        out_specs=vmem(1)[0],
        scratch_shapes=[
            pltpu.VMEM((slots, length + 2 * TILE), F32),
            pltpu.VMEM((seg_len + 2 * TILE, TILE), F32),
            pltpu.VMEM((TILE, TILE), F32),
        ]
        + [pltpu.VMEM((9 * SETS, TILE), F32)]
        + fir_scratch(seg_len, TILE),
        compiler_params=params(),
        cost_estimate=light(),
        name="whiten_slots",
    )(rows, traces, low, high, chan_taps, after)


def whiten_kernel(taps, rows, time_devs, x, low, high, sets, out, tall, *work):
    length = x.shape[1]
    half = (taps - 1) // 2
    here = lax.axis_index("tm")
    tall[0:TILE, :] = jnp.where(here > 0, low[...], 0.0).T
    tall[TILE + length :, :] = jnp.where(here < time_devs - 1, high[...], 0.0).T
    counts = set_sizes(taps)

    def turn(t, carry):
        start = pl.multiple_of(t * TILE, TILE)
        tall[pl.ds(start + TILE, TILE), :] = x[:, pl.ds(start, TILE)].T
        return carry

    lax.fori_loop(0, length // TILE, turn, 0)

    def block(i, carry):
        at = pl.multiple_of(i * rows, rows)
        out[pl.ds(at, rows), :] = fir(tall, sets, *work, at + TILE - half, rows, counts).astype(BF16)
        return carry

    lax.fori_loop(0, length // rows, block, 0)


def whiten(time_devs, taps, traces, low, high, sets):
    chans, length = traces.shape
    rows = 2 * TILE
    return pl.pallas_call(
        functools.partial(whiten_kernel, taps, rows, time_devs),
        out_shape=jax.ShapeDtypeStruct((length, chans), BF16),
        in_specs=vmem(4),
        out_specs=vmem(1)[0],
        scratch_shapes=[pltpu.VMEM((length + 2 * TILE, chans), F32)] + fir_scratch(rows, chans),
        compiler_params=params(),
        cost_estimate=light(),
        name="whiten",
    )(traces, low, high, sets)


def whiten_part_kernel(taps, rows, inner, sizes, x, sets, beside, _, *refs):
    outs, (tall, *work) = refs[:-4], refs[-4:]
    if inner:
        other, sources_row, *outs, full, wanted = outs
        choose_rows(sizes, x.shape[0], True, MOST, sources_row, wanted)
    length, size = x.shape[1], tall.shape[0] - 2 * TILE
    half = (taps - 1) // 2
    tiles = rows // TILE
    at_start = (lax.axis_index("tm") > 0) == inner
    start = jnp.where(at_start, 0, length - size)
    near = x[:, pl.ds(pl.multiple_of(jnp.where(at_start, size, length - size - TILE), TILE), TILE)]
    outside = beside[...] if inner else jnp.zeros_like(near)
    tall[0:TILE, :] = jnp.where(at_start, outside, near).T
    tall[TILE + size :, :] = jnp.where(at_start, near, outside).T
    counts = set_sizes(taps)

    def turn(t):
        tall[pl.ds(pl.multiple_of(t * TILE + TILE, TILE), TILE), :] = x[
            :, pl.ds(pl.multiple_of(start + t * TILE, TILE), TILE)
        ].T

    for t in range(tiles + 1):
        turn(t)

    if inner:
        edge = jnp.zeros((TILE, tall.shape[1]), BF16)
        full[0:TILE, :] = edge
        full[TILE + length :, :] = edge
        place = pl.multiple_of(TILE + jnp.where(at_start, size, 0), TILE)
        full[pl.ds(place, length - size), :] = other[...]
    done = 0
    for out in outs:

        def block(i, carry):
            at = pl.multiple_of(i * rows, rows)
            value = fir(tall, sets, *work, at + TILE - half, rows, counts).astype(BF16)
            out[pl.ds(at - done, rows), :] = value
            if inner:
                full[pl.ds(pl.multiple_of(TILE + start + at, TILE), rows), :] = value
            for t in range(tiles):
                turn(jnp.minimum((i + 1) * tiles + 1 + t, size // TILE - 1))
            return carry

        lax.fori_loop(done // rows, (done + out.shape[0]) // rows, block, 0)
        done += out.shape[0]


def whiten_part(taps, traces, sets, beside, after, pieces, inner, sizes, other=()):
    chans = traces.shape[0]
    size = sum(pieces)
    full = [traces.shape[1] + 2 * TILE] if inner else []
    extra = ()
    if inner:
        partners = other[1].shape[1]
        extra = (jax.ShapeDtypeStruct((partners, MOST * sizes[1] * sizes[2]), F32),)
    rows = 2 * TILE
    return pl.pallas_call(
        functools.partial(whiten_part_kernel, taps, rows, inner, sizes),
        out_shape=tuple(jax.ShapeDtypeStruct((piece, chans), BF16) for piece in (*pieces, *full)) + extra,
        in_specs=vmem(3) + [ANY] + vmem(len(other)),
        out_specs=tuple(vmem(len(pieces) + len(full) + len(extra))),
        scratch_shapes=[pltpu.VMEM((size + 2 * TILE, chans), F32)] + fir_scratch(rows, chans),
        compiler_params=params(),
        cost_estimate=light(),
        name="whiten_inner" if inner else "whiten_outer",
    )(traces, sets, beside, after, *other)


def order_kernel(ring, count, choose, after, *refs):
    parts, (*outs, gathered) = refs[:count], refs[count:]
    step = parts[0].shape[0]
    for i, part in enumerate(parts):
        gathered[i * step : (i + 1) * step, :] = part[...]
    if not ring:
        outs[0][...] = jnp.dot(choose[...].astype(BF16), gathered[...], preferred_element_type=F32).astype(BF16)
        return
    own, *sends = outs
    half, length = own.shape[0], sends[0].shape[1]
    here = lax.axis_index("tm")
    mine = choose[pl.ds(pl.multiple_of(here * half, half), half), :]
    few = half // 2
    other = (1 - here) * half + lax.axis_index("sub") * few
    theirs = choose[pl.ds(pl.multiple_of(other, few), few), :]
    wanted = jnp.concatenate([mine, theirs], 0).astype(BF16)
    got = jnp.dot(wanted, gathered[...], preferred_element_type=F32).astype(BF16)
    own[:, 0:TILE] = jnp.zeros((half, TILE), BF16)
    own[:, TILE + length :] = jnp.zeros((half, TILE), BF16)
    own[:, TILE : TILE + length] = got[:half]
    size = sends[0].shape[0]
    for n, send in enumerate(sends):
        send[...] = got[half + n * size : half + (n + 1) * size]


def order(choose, after, parts, ring):
    partners, total = choose.shape
    length = parts[0].shape[1]
    if ring:
        half = partners // 2
        out_shape = (
            jax.ShapeDtypeStruct((half, length + 2 * TILE), BF16),
            *[jax.ShapeDtypeStruct((half // ARRIVED, length), BF16)] * (ARRIVED // 2),
        )
        out_specs = tuple(vmem(1 + ARRIVED // 2))
    else:
        out_shape = jax.ShapeDtypeStruct((partners, length), BF16)
        out_specs = vmem(1)[0]
    return pl.pallas_call(
        functools.partial(order_kernel, ring, len(parts)),
        out_shape=out_shape,
        in_specs=vmem(1) + [ANY] + vmem(len(parts)),
        out_specs=out_specs,
        scratch_shapes=[pltpu.VMEM((total, length), BF16)],
        compiler_params=params(),
        cost_estimate=light(),
        name="order_partners",
    )(choose, after, *parts)


def lay_out(part, out, start, width):
    rows = part.shape[0]
    lane = lax.broadcasted_iota(jnp.int32, (rows, TILE), 1)
    tiles = [part[:, pl.ds(start + TILE * i, TILE)] for i in range(width // TILE + 1)]
    half = (LAGS - 1) // 2
    for b in range(FINE + 1):
        turned = [pltpu.roll(tile, half - b, 1) for tile in tiles]
        for i in range(width // TILE):
            piece = jnp.where(lane < half - b, turned[i], turned[i + 1])
            out[b * rows : (b + 1) * rows, TILE * i : TILE * i + TILE] = piece


def add_lags(shifted, chan, total, start, width, rows):
    chans = chan.shape[1]
    coarse = (LAGS - 1) // FINE
    pair = 2 if chans % TILE == 0 else 1
    for a in range(0, coarse, pair):
        cols = [chan[pl.ds(start + TILE - FINE * (a + i), width), :] for i in range(pair)]
        last = a + pair == coarse
        used = rows * (FINE + 1 if last else FINE)
        block = cols[0] if pair == 1 else jnp.concatenate(cols, 1)
        term = jnp.dot(shifted[:used, :], block, preferred_element_type=F32)
        for i in range(pair):
            size = used if i == pair - 1 else rows * FINE
            place = (a + i) * FINE * rows
            total[place : place + size, :] += term[:size, i * chans : (i + 1) * chans]


def correlate_all(part, chan, total, spare, start, width, chunk, rows):
    first, second, rest = spare
    whole = width // (2 * chunk) * (2 * chunk)
    lay_out(part, first, start, chunk)

    def advance(i, carry):
        now = pl.multiple_of(start + 2 * chunk * i, TILE)
        lay_out(part, second, now + chunk, chunk)
        add_lags(first, chan, total, now, chunk, rows)
        after = pl.multiple_of(jnp.minimum(now + 2 * chunk, start + whole - chunk), TILE)
        lay_out(part, first, after, chunk)
        add_lags(second, chan, total, now + chunk, chunk, rows)
        return carry

    lax.fori_loop(0, whole // (2 * chunk), advance, 0)
    if width > whole:
        lay_out(part, rest, start + whole, width - whole)
        add_lags(rest, chan, total, start + whole, width - whole, rows)


def add_pair(shifted, chan, before, total, start, width, rows, a, scale):
    chans = chan.shape[1]
    last = a + 2 == (LAGS - 1) // FINE
    used = rows * (FINE + 1 if last else FINE)
    term = None
    for copies, begin in zip(shifted, start):
        cols = [chan[pl.ds(begin + TILE - FINE * (a + i), width), :] for i in range(2)]
        piece = jnp.dot(copies[:used, :width], jnp.concatenate(cols, 1), preferred_element_type=F32)
        term = piece if term is None else term + piece
    for i in range(2):
        size = used if i == 1 else rows * FINE
        place = (a + i) * FINE * rows
        mine = term[:size, i * chans : (i + 1) * chans]
        if before is not None:
            mine = before[place : place + size, :] + mine
        total[place : place + size, :] = mine if scale is None else mine * scale


def correlate_ring(part, chan, total, spare, start, width, chunk, rows, ready, before, scale, out, sems):
    pairs = range(0, (LAGS - 1) // FINE, 2)
    rest = width % chunk
    count = width // chunk
    begin = [pl.multiple_of(start + rest + i * chunk, TILE) for i in range(count)]
    buffers = [spare[3] if rest and i == 0 else spare[i % 3] for i in range(count)]
    widths = [chunk + rest if i == 0 else chunk for i in range(count)]
    begin[0] = start
    lay_out(part, buffers[0], start, widths[0])
    for copy in ready:
        copy.wait()
    for i in range(count - 2):
        lay_out(part, buffers[i + 1], begin[i + 1], chunk)
        if i == count - 3:
            lay_out(part, buffers[i + 2], begin[i + 2], chunk)
        for a in pairs:
            add_pair([buffers[i]], chan, before, total, [begin[i]], widths[i], rows, a, None)
        before = total
    stores = []
    for n, a in enumerate(pairs):
        ends = (count - 2, count - 1)
        add_pair([buffers[i] for i in ends], chan, before, total, [begin[i] for i in ends], chunk, rows, a, scale)
        if out is not None:
            at = 2 * n * FINE * rows
            size = rows * (2 * FINE + (1 if a + 2 == (LAGS - 1) // FINE else 0))
            stores.append(pltpu.make_async_copy(total.at[pl.ds(at, size), :], out.at[pl.ds(at, size), :], sems.at[n]))
            stores[-1].start()
    for store in stores:
        store.wait()


def place_pieces(at_start, pieces, chan, length, sems):
    outer = pieces[0].shape[0]
    at = jnp.where(at_start, 0, length - outer)
    copies = []
    for n, piece in enumerate(pieces):
        size = piece.shape[0]
        to = chan.at[pl.ds(pl.multiple_of(TILE + at, TILE), size), :]
        copies.append(pltpu.make_async_copy(piece, to, sems.at[4 + n]))
        copies[-1].start()
        at = jnp.where(at_start, outer, 0) if n == 0 else at + size
    return copies


def first_kernel(chunk, part, chan, total, a, b, c, d):
    length = part.shape[1] - 2 * TILE
    start = pl.multiple_of(lax.axis_index("tm") * TILE, TILE)
    correlate_ring(part, chan, total, (a, b, c, d), start, length, chunk, part.shape[0], (), None, None, None, None)


def second_kernel(chunk, scale, count, own_part, *refs):
    arrived, (own_head, own_tail, before, *refs) = refs[:ARRIVED], refs[ARRIVED:]
    pieces, (out, total, part, chan, a, b, c, d, sems) = refs[:count], refs[count:]
    length = part.shape[1] - 2 * TILE
    rows = part.shape[0]
    here = lax.axis_index("tm")
    ready = place_pieces(here > 0, pieces, chan, length, sems)
    later = here > 0
    few = arrived[0].shape[0]
    core = lax.axis_index("sub")
    for n, piece in enumerate(arrived):
        n = n + core * ARRIVED // 2
        at = jnp.where(n < ARRIVED, n, n - ARRIVED) * few
        part[pl.ds(pl.multiple_of(at, few), few), TILE : TILE + length] = piece[...]
    part[:, 0:TILE] = jnp.where(later, 0, own_part[:, length : length + TILE]).astype(BF16)
    part[:, TILE + length :] = jnp.where(later, own_part[:, TILE : 2 * TILE], 0).astype(BF16)
    chan[0:TILE, :] = jnp.where(later, 0, own_tail[own_tail.shape[0] - TILE :, :]).astype(BF16)
    chan[TILE + length :, :] = jnp.where(later, own_head[0:TILE, :], 0).astype(BF16)
    correlate_ring(part, chan, total, (a, b, c, d), 0, length + TILE, chunk, rows, ready, before, scale, out, sems)


def whole_kernel(chunk, scale, part_in, chan_in, total, part, chan, a, b, c):
    length = chan_in.shape[0]
    rows = part.shape[0]
    part[:, 0:TILE] = jnp.zeros((rows, TILE), BF16)
    part[:, TILE + length :] = jnp.zeros((rows, TILE), BF16)
    part[:, TILE : TILE + length] = part_in[...]
    edge = jnp.zeros((TILE, chan.shape[1]), BF16)
    chan[0:TILE, :] = edge
    chan[TILE + length :, :] = edge
    chan[TILE : TILE + length, :] = chan_in[...]
    total[...] = jnp.zeros_like(total)
    correlate_all(part, chan, total, (a, b, c), 0, length + TILE, chunk, rows)
    total[...] = total[...] * scale


def spare(rows, widths):
    return [pltpu.VMEM((rows * (FINE + 1), width), BF16) for width in widths]


def shifted(array, axis, step):
    count = lax.axis_size(axis)
    return lax.ppermute(array, axis, [(i, (i + step) % count) for i in range(count)])


def on_device(traces, filters, sources):
    chans, length = traces.shape
    partners = sources.shape[0]
    sizes = tuple(lax.axis_size(axis) for axis in ("tm", "chan", "sub"))
    time_devs, chan_devs, sub_devs = sizes
    slots = min(chans, MOST)
    rows = partners // time_devs
    scale = 1.0 / math.sqrt(length * time_devs)
    chunk = 4 * TILE
    taps = filters.T
    ring = time_devs == 2 and sub_devs == 2 and chan_devs <= 4 and slots == MOST and chans % TILE == 0
    out_shape = jax.ShapeDtypeStruct((LAGS * rows, chans), F32)
    count = taps.shape[0]
    slot_rows, sets, chan_taps, held, *choose = prepare(sizes, sources, taps, traces, slots, ring)
    if ring:
        here = lax.axis_index("tm")
        edge = lax.dynamic_slice_in_dim(traces, jnp.where(here == 0, length - TILE, 0), TILE, 1)
        beside = shifted(edge, "tm", 1)
        far = length // 2
        outer = whiten_part(count, held, sets, edge, edge, (far,), False, sizes)
        beside, *outer = lax.optimization_barrier((beside, *outer))
        other_outer = [shifted(piece, "tm", 1) for piece in outer]
        picked = whiten_slots(sizes, count, slot_rows, held, beside, beside, chan_taps, outer[0], slots)
        *inner, own_chan, choose = whiten_part(count, held, sets, beside, picked, (length - far,), True, sizes, (*outer, sources.reshape(1, partners)))
        other_inner = [shifted(piece, "tm", 1) for piece in inner]
        mine = [picked] + [shifted(picked, "chan", step) for step in range(1, chan_devs)]
        theirs = [shifted(part, "sub", 1) for part in mine]
        own_part, *send = order(choose, other_outer[0], [*mine, *theirs], True)
        near_rows = [shifted(part, "tm", 1) for part in send]
        pieces = len(outer) + len(inner)
        before = pl.pallas_call(
            functools.partial(first_kernel, chunk),
            out_shape=out_shape,
            in_specs=vmem(2),
            out_specs=vmem(1)[0],
            scratch_shapes=spare(rows, (chunk, chunk, chunk, chunk + TILE)),
            compiler_params=params(),
            cost_estimate=light(),
            name="correlate_own",
        )(own_part, own_chan)
        near_rows, other_inner, before = lax.optimization_barrier((near_rows, other_inner, before))
        far_rows = [shifted(part, "sub", 1) for part in near_rows]
        total = pl.pallas_call(
            functools.partial(second_kernel, chunk, scale, pieces),
            out_shape=out_shape,
            in_specs=vmem(4 + 2 * len(send)) + [ANY] * pieces,
            out_specs=ANY,
            scratch_shapes=[
                pltpu.VMEM(out_shape.shape, F32),
                pltpu.VMEM((rows, length + 2 * TILE), BF16),
                pltpu.VMEM((length + 2 * TILE, chans), BF16),
            ]
            + spare(rows, (chunk, chunk, chunk, chunk + TILE))
            + [pltpu.SemaphoreType.DMA((4 + pieces,))],
            compiler_params=params(),
            cost_estimate=light(),
            name="correlate_other",
        )(own_part, *near_rows, *far_rows, inner[0], inner[-1], before, *other_outer, *other_inner)
    else:
        low = lax.ppermute(traces[:, length - TILE :], "tm", [(i, i + 1) for i in range(time_devs - 1)])
        high = lax.ppermute(traces[:, :TILE], "tm", [(i + 1, i) for i in range(time_devs - 1)])
        picked = whiten_slots(sizes, count, slot_rows, held, low, high, chan_taps, low, slots)
        whitened = whiten(time_devs, count, traces, low, high, sets)
        gathered = lax.all_gather(picked, ("chan", "sub"), axis=0, tiled=True)
        all_parts = order(choose[0], low, [gathered], False)
        parts = lax.all_to_all(all_parts, "tm", 0, 1, tiled=True)
        all_chans = lax.all_gather(whitened, "tm", axis=0, tiled=True)
        full = length * time_devs
        total = pl.pallas_call(
            functools.partial(whole_kernel, chunk, scale),
            out_shape=out_shape,
            in_specs=vmem(2),
            out_specs=vmem(1)[0],
            scratch_shapes=[
                pltpu.VMEM((rows, full + 2 * TILE), BF16),
                pltpu.VMEM((full + 2 * TILE, chans), BF16),
            ]
            + spare(rows, (chunk, chunk, TILE)),
            compiler_params=pltpu.CompilerParams(vmem_limit_bytes=2 * VMEM_BYTES),
            name="correlate_whole",
        )(parts, all_chans)
    return jnp.transpose(total.reshape(LAGS, rows, chans), (1, 0, 2))


def solution(mesh):
    return jax.shard_map(
        on_device,
        mesh=mesh,
        in_specs=(
            P(("groups", "chan", "sub"), "tm"),
            P(("groups", "chan", "sub"), None),
            P("groups"),
        ),
        out_specs=P("tm", None, ("groups", "chan", "sub")),
        check_vma=False,
    )
```

```python
import functools
import math

import jax
import jax.numpy as jnp
from jax import lax
from jax.experimental import pallas as pl
from jax.experimental.pallas import tpu as pltpu
from jax.sharding import PartitionSpec as P

LAGS = 129
MOST = 16
TILE = 128
FINE = 16
SETS = 24
ARRIVED = 2
F32 = jnp.float32
BF16 = jnp.bfloat16
VMEM_BYTES = 24 * 2**20


def vmem(count):
    return [pl.BlockSpec(memory_space=pltpu.VMEM)] * count


SMEM = pl.BlockSpec(memory_space=pltpu.SMEM)
ANY = pl.BlockSpec(memory_space=pl.ANY)


def params():
    return pltpu.CompilerParams(vmem_limit_bytes=VMEM_BYTES)


def light():
    return pl.CostEstimate(flops=1000, bytes_accessed=1000, transcendentals=0)


def set_sizes(taps):
    sizes = []
    for group in ((taps + 1) // 2, taps // 2, (taps + 1) // 2):
        sizes += [(group + 1) // 2, group // 2, (group + 1) // 2]
    return sizes


def split_taps(filters, sets, taps):
    def take(rows):
        return [filters[k : k + 1, :] if k < taps else None for k in rows]

    def plus(a, b):
        return [x if y is None else (y if x is None else x + y) for x, y in zip(a, b)]

    whole = 2 * ((taps + 1) // 2)
    even, odd = take(range(0, whole, 2)), take(range(1, whole, 2))
    for i, group in enumerate((even, odd, plus(even, odd))):
        group = group + [None] * (len(group) % 2)
        first, second = group[0::2], group[1::2]
        for j, rows in enumerate((first, second, plus(first, second))):
            for k, row in enumerate(rows):
                if row is not None:
                    at = SETS * (3 * i + j) + k
                    sets[at : at + 1, :] = row


def part_fir(stage, at, sets, row, count, rows):
    total = None
    for first in range(8):
        later = [j for j in range((count + 7) // 8) if first + 8 * j < count]
        window = stage[at + first : at + first + rows + 8 * later[-1], :]
        for j in later:
            k = row + first + 8 * j
            term = sets[k : k + 1, :] * window[8 * j : 8 * j + rows]
            total = term if total is None else total + term
    return total


def fir(samples, sets, stage, late, mixed, base, rows, counts):
    few = rows // 4
    extent = few + 32
    x3, x4, x5, x6 = (samples[pl.ds(base - 32 + p, extent, stride=4), :] for p in (3, 4, 5, 6))
    arrays = (x6, x4, x6 + x4, x5, x3, x5 + x3, x6 + x5, x4 + x3, (x6 + x4) + (x5 + x3))
    for i, array in enumerate(arrays):
        stage[i * extent : (i + 1) * extent, :] = array

    def halves(i, lead):
        size = few + lead
        at = 3 * i * extent
        p0 = part_fir(stage, at, sets, SETS * 3 * i, counts[3 * i], few + 8)
        p1 = part_fir(stage, at + extent + 8 - lead, sets, SETS * (3 * i + 1), counts[3 * i + 1], size)
        p2 = part_fir(stage, at + 2 * extent + 8 - lead, sets, SETS * (3 * i + 2), counts[3 * i + 2], size)
        late[8 : 16 + few, :] = p0
        return late[15 - lead : 15 - lead + size, :] + p1, p2 - p1 - late[16 - lead : 16 - lead + size, :]

    a_even, a_odd = halves(0, 8)
    b_even, b_odd = halves(1, 0)
    c_even, c_odd = halves(2, 0)
    mixed[0 : few + 8, :] = a_odd
    y0 = mixed[7 : 7 + few, :] + b_even
    y1 = c_even - a_even[8:] - b_even
    y2 = a_even[8:] + b_odd
    y3 = c_odd - a_odd[8:] - b_odd
    for p, y in enumerate((y0, y1, y2, y3)):
        mixed[pl.ds(p, few, stride=4), :] = y
    return mixed[0:rows, :]


def fir_scratch(rows, lanes):
    few = rows // 4
    return [
        pltpu.VMEM((9 * (few + 32), lanes), F32),
        pltpu.VMEM((few + 16, lanes), F32),
        pltpu.VMEM((max(rows, few + 8), lanes), F32),
    ]


def place_of(axes, sizes):
    at = 0
    for axis, size in zip(axes, sizes):
        at = at * size + lax.axis_index(axis)
    return at


def choose_rows(sizes, chans, ring, slots, sources_row, wanted):
    partners = sources_row.shape[1]
    _, chan_devs, sub_devs = sizes
    own_row = jnp.broadcast_to(sources_row[...].astype(F32), (partners, partners))
    owner_row = jnp.floor((own_row + 0.5) * (1.0 / chans))
    owner_col = owner_row.T
    lane = lax.broadcasted_iota(jnp.int32, (partners, partners), 1)
    line = lax.broadcasted_iota(jnp.int32, (partners, partners), 0)
    earlier = (owner_row == owner_col) & (lane < line)
    rank = jnp.sum(earlier.astype(F32), axis=1, keepdims=True)
    owner = owner_col[:, 0:1]
    if ring:
        owner_chan = jnp.floor((owner + 0.5) * (1.0 / sub_devs))
        owner_sub = owner - sub_devs * owner_chan
        my_chan = lax.axis_index("chan").astype(F32)
        my_sub = lax.axis_index("sub").astype(F32)
        behind = my_chan - owner_chan
        behind = jnp.where(behind < 0, behind + chan_devs, behind)
        place = jnp.where(owner_sub == my_sub, 0.0, 1.0) * chan_devs + behind
    else:
        place = owner
    at = lax.broadcasted_iota(jnp.int32, wanted.shape, 1).astype(F32)
    wanted[...] = (place * slots + rank == at).astype(F32)


def prepare_kernel(sizes, chans, ring, slots, sources_row, filters, _, sets, chan_taps, same, *wanted):
    taps = filters.shape[0]
    split_taps(filters, sets, taps)
    chan_taps[...] = jnp.concatenate([filters[...], jnp.zeros((TILE - taps, chans), F32)], 0).T
    if not ring:
        choose_rows(sizes, chans, ring, slots, sources_row, wanted[0])


def prepare(sizes, sources, filters, traces, slots, ring):
    taps, chans = filters.shape
    partners = sources.shape[0]
    total = slots * sizes[1] * sizes[2]
    return pl.pallas_call(
        functools.partial(prepare_kernel, sizes, chans, ring, slots),
        out_shape=(
            jax.ShapeDtypeStruct((9 * SETS, chans), F32),
            jax.ShapeDtypeStruct((chans, TILE), F32),
            jax.ShapeDtypeStruct(traces.shape, F32),
            *[jax.ShapeDtypeStruct((partners, total), F32)] * (not ring),
        ),
        in_specs=vmem(2) + [ANY],
        out_specs=(*vmem(2), ANY, *vmem(not ring)),
        input_output_aliases={2: 2},
        compiler_params=params(),
        cost_estimate=light(),
        name="prepare",
    )(sources.reshape(1, partners), filters, traces)


def slots_kernel(taps, sizes, sources, x, low, high, chan_taps, after, out, rows, wide, tall, lane_taps, *work):
    chans, length = x.shape
    slots = out.shape[0]
    segs = TILE // slots
    seg_len = length // segs
    half = (taps - 1) // 2
    first_chan = place_of(("chan", "sub"), sizes[1:]) * chans
    for s in range(slots):
        rows[s] = 0

    def find(p, count):
        local = sources[p] - first_chan
        mine = (local >= 0) & (local < chans)
        rows[jnp.where(mine, count, slots)] = local
        return count + mine.astype(jnp.int32)

    lax.fori_loop(0, sources.shape[0], find, 0, unroll=16)
    here = lax.axis_index("tm")
    keep_low = (here > 0).astype(F32)
    keep_high = (here < sizes[0] - 1).astype(F32)
    for s in range(slots):
        row = rows[s]
        group = pl.multiple_of((row >> 3) << 3, 8)
        turn = (s - row) & 7

        def pick(ref):
            return pltpu.roll(ref[pl.ds(group, 8), :], turn, 0)[s % 8 : s % 8 + 1, :]

        wide[s : s + 1, 0:TILE] = pick(low) * keep_low
        wide[s : s + 1, TILE : TILE + length] = pick(x)
        wide[s : s + 1, TILE + length :] = pick(high) * keep_high
        lane_taps[s : s + 1, :] = pick(chan_taps)
    picked = lane_taps[0:slots, :]
    lane_taps[...] = jnp.concatenate([picked] * segs, 0).T
    for t in range(seg_len // TILE + 2):
        cols = [wide[:, g * seg_len + t * TILE : g * seg_len + (t + 1) * TILE] for g in range(segs)]
        tall[t * TILE : (t + 1) * TILE, :] = jnp.concatenate(cols, 0).T
    split_taps(lane_taps, work[0], taps)
    counts = set_sizes(taps)
    done = fir(tall, *work, TILE - half, seg_len, counts)
    for t in range(seg_len // TILE):
        turned = done[t * TILE : (t + 1) * TILE].T
        for g in range(segs):
            start = g * seg_len + t * TILE
            out[:, start : start + TILE] = turned[g * slots : (g + 1) * slots].astype(BF16)


def whiten_slots(sizes, taps, rows, traces, low, high, chan_taps, after, slots):
    length = traces.shape[1]
    seg_len = length * slots // TILE
    return pl.pallas_call(
        functools.partial(slots_kernel, taps, sizes),
        out_shape=jax.ShapeDtypeStruct((slots, length), BF16),
        in_specs=[SMEM] + vmem(4) + [ANY],
        out_specs=vmem(1)[0],
        scratch_shapes=[
            pltpu.SMEM((slots + 1,), jnp.int32),
            pltpu.VMEM((slots, length + 2 * TILE), F32),
            pltpu.VMEM((seg_len + 2 * TILE, TILE), F32),
            pltpu.VMEM((TILE, TILE), F32),
        ]
        + [pltpu.VMEM((9 * SETS, TILE), F32)]
        + fir_scratch(seg_len, TILE),
        compiler_params=params(),
        cost_estimate=light(),
        name="whiten_slots",
    )(rows, traces, low, high, chan_taps, after)


def whiten_kernel(taps, rows, time_devs, x, low, high, sets, out, tall, *work):
    length = x.shape[1]
    half = (taps - 1) // 2
    here = lax.axis_index("tm")
    tall[0:TILE, :] = jnp.where(here > 0, low[...], 0.0).T
    tall[TILE + length :, :] = jnp.where(here < time_devs - 1, high[...], 0.0).T
    counts = set_sizes(taps)

    def turn(t, carry):
        start = pl.multiple_of(t * TILE, TILE)
        tall[pl.ds(start + TILE, TILE), :] = x[:, pl.ds(start, TILE)].T
        return carry

    lax.fori_loop(0, length // TILE, turn, 0)

    def block(i, carry):
        at = pl.multiple_of(i * rows, rows)
        out[pl.ds(at, rows), :] = fir(tall, sets, *work, at + TILE - half, rows, counts).astype(BF16)
        return carry

    lax.fori_loop(0, length // rows, block, 0)


def whiten(time_devs, taps, traces, low, high, sets):
    chans, length = traces.shape
    rows = 2 * TILE
    return pl.pallas_call(
        functools.partial(whiten_kernel, taps, rows, time_devs),
        out_shape=jax.ShapeDtypeStruct((length, chans), BF16),
        in_specs=vmem(4),
        out_specs=vmem(1)[0],
        scratch_shapes=[pltpu.VMEM((length + 2 * TILE, chans), F32)] + fir_scratch(rows, chans),
        compiler_params=params(),
        cost_estimate=light(),
        name="whiten",
    )(traces, low, high, sets)


def whiten_part_kernel(taps, rows, inner, sizes, x, sets, beside, _, *refs):
    outs, (tall, *work) = refs[:-4], refs[-4:]
    if inner:
        other, sources_row, *outs, full, wanted = outs
        choose_rows(sizes, x.shape[0], True, MOST, sources_row, wanted)
    length, size = x.shape[1], tall.shape[0] - 2 * TILE
    half = (taps - 1) // 2
    tiles = rows // TILE
    at_start = (lax.axis_index("tm") > 0) == inner
    start = jnp.where(at_start, 0, length - size)
    near = x[:, pl.ds(pl.multiple_of(jnp.where(at_start, size, length - size - TILE), TILE), TILE)]
    outside = beside[...] if inner else jnp.zeros_like(near)
    tall[0:TILE, :] = jnp.where(at_start, outside, near).T
    tall[TILE + size :, :] = jnp.where(at_start, near, outside).T
    counts = set_sizes(taps)

    def turn(t):
        tall[pl.ds(pl.multiple_of(t * TILE + TILE, TILE), TILE), :] = x[
            :, pl.ds(pl.multiple_of(start + t * TILE, TILE), TILE)
        ].T

    for t in range(tiles + 1):
        turn(t)

    if inner:
        edge = jnp.zeros((TILE, tall.shape[1]), BF16)
        full[0:TILE, :] = edge
        full[TILE + length :, :] = edge
        place = pl.multiple_of(TILE + jnp.where(at_start, size, 0), TILE)
        full[pl.ds(place, length - size), :] = other[...]
    done = 0
    for out in outs:

        def block(i, carry):
            at = pl.multiple_of(i * rows, rows)
            value = fir(tall, sets, *work, at + TILE - half, rows, counts).astype(BF16)
            out[pl.ds(at - done, rows), :] = value
            if inner:
                full[pl.ds(pl.multiple_of(TILE + start + at, TILE), rows), :] = value
            for t in range(tiles):
                turn(jnp.minimum((i + 1) * tiles + 1 + t, size // TILE - 1))
            return carry

        lax.fori_loop(done // rows, (done + out.shape[0]) // rows, block, 0)
        done += out.shape[0]


def whiten_part(taps, traces, sets, beside, after, pieces, inner, sizes, other=()):
    chans = traces.shape[0]
    size = sum(pieces)
    full = [traces.shape[1] + 2 * TILE] if inner else []
    extra = ()
    if inner:
        partners = other[1].shape[1]
        extra = (jax.ShapeDtypeStruct((partners, MOST * sizes[1] * sizes[2]), F32),)
    rows = 2 * TILE
    return pl.pallas_call(
        functools.partial(whiten_part_kernel, taps, rows, inner, sizes),
        out_shape=tuple(jax.ShapeDtypeStruct((piece, chans), BF16) for piece in (*pieces, *full)) + extra,
        in_specs=vmem(3) + [ANY] + vmem(len(other)),
        out_specs=tuple(vmem(len(pieces) + len(full) + len(extra))),
        scratch_shapes=[pltpu.VMEM((size + 2 * TILE, chans), F32)] + fir_scratch(rows, chans),
        compiler_params=params(),
        cost_estimate=light(),
        name="whiten_inner" if inner else "whiten_outer",
    )(traces, sets, beside, after, *other)


def order_kernel(ring, count, choose, after, *refs):
    parts, (*outs, gathered) = refs[:count], refs[count:]
    step = parts[0].shape[0]
    for i, part in enumerate(parts):
        gathered[i * step : (i + 1) * step, :] = part[...]
    if not ring:
        outs[0][...] = jnp.dot(choose[...].astype(BF16), gathered[...], preferred_element_type=F32).astype(BF16)
        return
    own, *sends = outs
    half, length = own.shape[0], sends[0].shape[1]
    here = lax.axis_index("tm")
    mine = choose[pl.ds(pl.multiple_of(here * half, half), half), :]
    few = half // 2
    other = (1 - here) * half + lax.axis_index("sub") * few
    theirs = choose[pl.ds(pl.multiple_of(other, few), few), :]
    wanted = jnp.concatenate([mine, theirs], 0).astype(BF16)
    got = jnp.dot(wanted, gathered[...], preferred_element_type=F32).astype(BF16)
    own[:, 0:TILE] = jnp.zeros((half, TILE), BF16)
    own[:, TILE + length :] = jnp.zeros((half, TILE), BF16)
    own[:, TILE : TILE + length] = got[:half]
    size = sends[0].shape[0]
    for n, send in enumerate(sends):
        send[...] = got[half + n * size : half + (n + 1) * size]


def order(choose, after, parts, ring):
    partners, total = choose.shape
    length = parts[0].shape[1]
    if ring:
        half = partners // 2
        out_shape = (
            jax.ShapeDtypeStruct((half, length + 2 * TILE), BF16),
            *[jax.ShapeDtypeStruct((half // ARRIVED, length), BF16)] * (ARRIVED // 2),
        )
        out_specs = tuple(vmem(1 + ARRIVED // 2))
    else:
        out_shape = jax.ShapeDtypeStruct((partners, length), BF16)
        out_specs = vmem(1)[0]
    return pl.pallas_call(
        functools.partial(order_kernel, ring, len(parts)),
        out_shape=out_shape,
        in_specs=vmem(1) + [ANY] + vmem(len(parts)),
        out_specs=out_specs,
        scratch_shapes=[pltpu.VMEM((total, length), BF16)],
        compiler_params=params(),
        cost_estimate=light(),
        name="order_partners",
    )(choose, after, *parts)


def lay_out(part, out, start, width):
    rows = part.shape[0]
    lane = lax.broadcasted_iota(jnp.int32, (rows, TILE), 1)
    tiles = [part[:, pl.ds(start + TILE * i, TILE)] for i in range(width // TILE + 1)]
    half = (LAGS - 1) // 2
    for b in range(FINE + 1):
        turned = [pltpu.roll(tile, half - b, 1) for tile in tiles]
        for i in range(width // TILE):
            piece = jnp.where(lane < half - b, turned[i], turned[i + 1])
            out[b * rows : (b + 1) * rows, TILE * i : TILE * i + TILE] = piece


def add_lags(shifted, chan, total, start, width, rows):
    chans = chan.shape[1]
    coarse = (LAGS - 1) // FINE
    pair = 2 if chans % TILE == 0 else 1
    for a in range(0, coarse, pair):
        cols = [chan[pl.ds(start + TILE - FINE * (a + i), width), :] for i in range(pair)]
        last = a + pair == coarse
        used = rows * (FINE + 1 if last else FINE)
        block = cols[0] if pair == 1 else jnp.concatenate(cols, 1)
        term = jnp.dot(shifted[:used, :], block, preferred_element_type=F32)
        for i in range(pair):
            size = used if i == pair - 1 else rows * FINE
            place = (a + i) * FINE * rows
            total[place : place + size, :] += term[:size, i * chans : (i + 1) * chans]


def correlate_all(part, chan, total, spare, start, width, chunk, rows):
    first, second, rest = spare
    whole = width // (2 * chunk) * (2 * chunk)
    lay_out(part, first, start, chunk)

    def advance(i, carry):
        now = pl.multiple_of(start + 2 * chunk * i, TILE)
        lay_out(part, second, now + chunk, chunk)
        add_lags(first, chan, total, now, chunk, rows)
        after = pl.multiple_of(jnp.minimum(now + 2 * chunk, start + whole - chunk), TILE)
        lay_out(part, first, after, chunk)
        add_lags(second, chan, total, now + chunk, chunk, rows)
        return carry

    lax.fori_loop(0, whole // (2 * chunk), advance, 0)
    if width > whole:
        lay_out(part, rest, start + whole, width - whole)
        add_lags(rest, chan, total, start + whole, width - whole, rows)


def add_pair(shifted, chan, before, total, start, width, rows, a, scale):
    chans = chan.shape[1]
    last = a + 2 == (LAGS - 1) // FINE
    used = rows * (FINE + 1 if last else FINE)
    term = None
    for copies, begin in zip(shifted, start):
        cols = [chan[pl.ds(begin + TILE - FINE * (a + i), width), :] for i in range(2)]
        piece = jnp.dot(copies[:used, :width], jnp.concatenate(cols, 1), preferred_element_type=F32)
        term = piece if term is None else term + piece
    for i in range(2):
        size = used if i == 1 else rows * FINE
        place = (a + i) * FINE * rows
        mine = term[:size, i * chans : (i + 1) * chans]
        if before is not None:
            mine = before[place : place + size, :] + mine
        total[place : place + size, :] = mine if scale is None else mine * scale


def correlate_ring(part, chan, total, spare, start, width, chunk, rows, ready, before, scale, out, sems):
    pairs = range(0, (LAGS - 1) // FINE, 2)
    rest = width % chunk
    count = width // chunk
    begin = [pl.multiple_of(start + rest + i * chunk, TILE) for i in range(count)]
    buffers = [spare[3] if rest and i == 0 else spare[i % 3] for i in range(count)]
    widths = [chunk + rest if i == 0 else chunk for i in range(count)]
    begin[0] = start
    lay_out(part, buffers[0], start, widths[0])
    for copy in ready:
        copy.wait()
    for i in range(count - 2):
        lay_out(part, buffers[i + 1], begin[i + 1], chunk)
        if i == count - 3:
            lay_out(part, buffers[i + 2], begin[i + 2], chunk)
        for a in pairs:
            add_pair([buffers[i]], chan, before, total, [begin[i]], widths[i], rows, a, None)
        before = total
    stores = []
    for n, a in enumerate(pairs):
        ends = (count - 2, count - 1)
        add_pair([buffers[i] for i in ends], chan, before, total, [begin[i] for i in ends], chunk, rows, a, scale)
        if out is not None:
            at = 2 * n * FINE * rows
            size = rows * (2 * FINE + (1 if a + 2 == (LAGS - 1) // FINE else 0))
            stores.append(pltpu.make_async_copy(total.at[pl.ds(at, size), :], out.at[pl.ds(at, size), :], sems.at[n]))
            stores[-1].start()
    for store in stores:
        store.wait()


def place_pieces(at_start, pieces, chan, length, sems):
    outer = pieces[0].shape[0]
    at = jnp.where(at_start, 0, length - outer)
    copies = []
    for n, piece in enumerate(pieces):
        size = piece.shape[0]
        to = chan.at[pl.ds(pl.multiple_of(TILE + at, TILE), size), :]
        copies.append(pltpu.make_async_copy(piece, to, sems.at[4 + n]))
        copies[-1].start()
        at = jnp.where(at_start, outer, 0) if n == 0 else at + size
    return copies


def first_kernel(chunk, part, chan, total, a, b, c, d):
    length = part.shape[1] - 2 * TILE
    start = pl.multiple_of(lax.axis_index("tm") * TILE, TILE)
    correlate_ring(part, chan, total, (a, b, c, d), start, length, chunk, part.shape[0], (), None, None, None, None)


def second_kernel(chunk, scale, count, own_part, *refs):
    arrived, (own_head, own_tail, before, *refs) = refs[:ARRIVED], refs[ARRIVED:]
    pieces, (out, total, part, chan, a, b, c, d, sems) = refs[:count], refs[count:]
    length = part.shape[1] - 2 * TILE
    rows = part.shape[0]
    here = lax.axis_index("tm")
    ready = place_pieces(here > 0, pieces, chan, length, sems)
    later = here > 0
    few = arrived[0].shape[0]
    core = lax.axis_index("sub")
    for n, piece in enumerate(arrived):
        n = n + core * ARRIVED // 2
        at = jnp.where(n < ARRIVED, n, n - ARRIVED) * few
        part[pl.ds(pl.multiple_of(at, few), few), TILE : TILE + length] = piece[...]
    part[:, 0:TILE] = jnp.where(later, 0, own_part[:, length : length + TILE]).astype(BF16)
    part[:, TILE + length :] = jnp.where(later, own_part[:, TILE : 2 * TILE], 0).astype(BF16)
    chan[0:TILE, :] = jnp.where(later, 0, own_tail[own_tail.shape[0] - TILE :, :]).astype(BF16)
    chan[TILE + length :, :] = jnp.where(later, own_head[0:TILE, :], 0).astype(BF16)
    correlate_ring(part, chan, total, (a, b, c, d), 0, length + TILE, chunk, rows, ready, before, scale, out, sems)


def whole_kernel(chunk, scale, part_in, chan_in, total, part, chan, a, b, c):
    length = chan_in.shape[0]
    rows = part.shape[0]
    part[:, 0:TILE] = jnp.zeros((rows, TILE), BF16)
    part[:, TILE + length :] = jnp.zeros((rows, TILE), BF16)
    part[:, TILE : TILE + length] = part_in[...]
    edge = jnp.zeros((TILE, chan.shape[1]), BF16)
    chan[0:TILE, :] = edge
    chan[TILE + length :, :] = edge
    chan[TILE : TILE + length, :] = chan_in[...]
    total[...] = jnp.zeros_like(total)
    correlate_all(part, chan, total, (a, b, c), 0, length + TILE, chunk, rows)
    total[...] = total[...] * scale


def spare(rows, widths):
    return [pltpu.VMEM((rows * (FINE + 1), width), BF16) for width in widths]


def shifted(array, axis, step):
    count = lax.axis_size(axis)
    return lax.ppermute(array, axis, [(i, (i + step) % count) for i in range(count)])


def on_device(traces, filters, sources):
    chans, length = traces.shape
    partners = sources.shape[0]
    sizes = tuple(lax.axis_size(axis) for axis in ("tm", "chan", "sub"))
    time_devs, chan_devs, sub_devs = sizes
    slots = min(chans, MOST)
    rows = partners // time_devs
    scale = 1.0 / math.sqrt(length * time_devs)
    chunk = 4 * TILE
    taps = filters.T
    ring = time_devs == 2 and sub_devs == 2 and chan_devs <= 4 and slots == MOST and chans % TILE == 0
    out_shape = jax.ShapeDtypeStruct((LAGS * rows, chans), F32)
    count = taps.shape[0]
    sets, chan_taps, held, *choose = prepare(sizes, sources, taps, traces, slots, ring)
    if ring:
        here = lax.axis_index("tm")
        edge = lax.dynamic_slice_in_dim(traces, jnp.where(here == 0, length - TILE, 0), TILE, 1)
        beside = shifted(edge, "tm", 1)
        far = length // 2
        outer = whiten_part(count, held, sets, edge, edge, (far,), False, sizes)
        beside, *outer = lax.optimization_barrier((beside, *outer))
        other_outer = [shifted(piece, "tm", 1) for piece in outer]
        picked = whiten_slots(sizes, count, sources, held, beside, beside, chan_taps, outer[0], slots)
        *inner, own_chan, choose = whiten_part(count, held, sets, beside, picked, (length - far,), True, sizes, (*outer, sources.reshape(1, partners)))
        other_inner = [shifted(piece, "tm", 1) for piece in inner]
        mine = [picked] + [shifted(picked, "chan", step) for step in range(1, chan_devs)]
        theirs = [shifted(part, "sub", 1) for part in mine]
        own_part, *send = order(choose, other_outer[0], [*mine, *theirs], True)
        near_rows = [shifted(part, "tm", 1) for part in send]
        pieces = len(outer) + len(inner)
        before = pl.pallas_call(
            functools.partial(first_kernel, chunk),
            out_shape=out_shape,
            in_specs=vmem(2),
            out_specs=vmem(1)[0],
            scratch_shapes=spare(rows, (chunk, chunk, chunk, chunk + TILE)),
            compiler_params=params(),
            cost_estimate=light(),
            name="correlate_own",
        )(own_part, own_chan)
        near_rows, other_inner, before = lax.optimization_barrier((near_rows, other_inner, before))
        far_rows = [shifted(part, "sub", 1) for part in near_rows]
        total = pl.pallas_call(
            functools.partial(second_kernel, chunk, scale, pieces),
            out_shape=out_shape,
            in_specs=vmem(4 + 2 * len(send)) + [ANY] * pieces,
            out_specs=ANY,
            scratch_shapes=[
                pltpu.VMEM(out_shape.shape, F32),
                pltpu.VMEM((rows, length + 2 * TILE), BF16),
                pltpu.VMEM((length + 2 * TILE, chans), BF16),
            ]
            + spare(rows, (chunk, chunk, chunk, chunk + TILE))
            + [pltpu.SemaphoreType.DMA((4 + pieces,))],
            compiler_params=params(),
            cost_estimate=light(),
            name="correlate_other",
        )(own_part, *near_rows, *far_rows, inner[0], inner[-1], before, *other_outer, *other_inner)
    else:
        low = lax.ppermute(traces[:, length - TILE :], "tm", [(i, i + 1) for i in range(time_devs - 1)])
        high = lax.ppermute(traces[:, :TILE], "tm", [(i + 1, i) for i in range(time_devs - 1)])
        picked = whiten_slots(sizes, count, sources, held, low, high, chan_taps, low, slots)
        whitened = whiten(time_devs, count, traces, low, high, sets)
        gathered = lax.all_gather(picked, ("chan", "sub"), axis=0, tiled=True)
        all_parts = order(choose[0], low, [gathered], False)
        parts = lax.all_to_all(all_parts, "tm", 0, 1, tiled=True)
        all_chans = lax.all_gather(whitened, "tm", axis=0, tiled=True)
        full = length * time_devs
        total = pl.pallas_call(
            functools.partial(whole_kernel, chunk, scale),
            out_shape=out_shape,
            in_specs=vmem(2),
            out_specs=vmem(1)[0],
            scratch_shapes=[
                pltpu.VMEM((rows, full + 2 * TILE), BF16),
                pltpu.VMEM((full + 2 * TILE, chans), BF16),
            ]
            + spare(rows, (chunk, chunk, TILE)),
            compiler_params=pltpu.CompilerParams(vmem_limit_bytes=2 * VMEM_BYTES),
            name="correlate_whole",
        )(parts, all_chans)
    return jnp.transpose(total.reshape(LAGS, rows, chans), (1, 0, 2))


def solution(mesh):
    return jax.shard_map(
        on_device,
        mesh=mesh,
        in_specs=(
            P(("groups", "chan", "sub"), "tm"),
            P(("groups", "chan", "sub"), None),
            P("groups"),
        ),
        out_specs=P("tm", None, ("groups", "chan", "sub")),
        check_vma=False,
    )
```
